256 devices in a mesh: row: 8 (over y, z_hi), col: 8 (over z_lo, core), depth: 4 (over x).
Axes of the slice: x: 4, y: 4, z: 8 (z_hi: 2, z_lo: 4; z = z_hi * 4 + z_lo), core: 2. Of those that a mesh axis runs over, the one named last changes fastest.
Arguments:
- left_tiles: float32 [8, 8, 4, 32, 4096], P('row', 'col', 'depth'), may hold values from -2 to 2
- right_tiles: float32 [8, 8, 4, 1, 32, 4096], P('row', 'col', 'depth'), may hold values from -2 to 2
- square_tiles: float32 [8, 8, 128, 4096], P('row', 'col', 'depth'), may hold values from -4 to 4
- pairs: int32 [8, 8, 4, 8, 3, 64], P('row', 'col', 'depth'), may hold values from 0 to 127, as said below
- counts: int32 [8, 8, 4, 8], P('row', 'col', 'depth'), may hold values from 1 to 64
Outputs:
- purified: float32 [8, 8, 128, 4096], P('row', 'col', 'depth')
The draws below stay inside these ranges and needn't reach their ends.
Inputs may be any that keep to these rules, and one draw needn't show every extreme that they name: pairs[..., 0, :] lies below 32, pairs[..., 1, :] below 32, pairs[..., 2, :] below 128; entries at or beyond the count are padding with valid slots.
All inputs are finite; a program needn't handle non-finite values.
Results may differ from the reference program's by a relative error of at most 0.0003.
Values sent between devices are 32-bit elements; how exact they have to be, the bound alone decides.
No kernel may reach another device: no remote copies, remote signals or barrier semaphores. Data moves between devices by JAX's collectives and lax.ppermute only.
A program may use at most 64 MiB of HBM per device.

```python
import jax
import jax.numpy as jnp
from jax import lax

TILE_EDGE = 64
LEFT_SLOTS = 32
RIGHT_SLOTS = 32
PRODUCTS = 64
GRID_ROWS = 8
GRID_COLS = 8
LAYERS = 4
CANNON_STEPS = 8
PANEL_QUEUE = 1
TOTAL_SLOTS = 128


def draw_pairs(key, part):
    key = jax.random.fold_in(key, 11)
    first, second, third = jax.random.split(key, 3)
    shape = (GRID_ROWS, GRID_COLS, LAYERS, CANNON_STEPS, PRODUCTS)
    left_slot = jax.random.randint(first, shape, 0, LEFT_SLOTS)
    right_slot = jax.random.randint(second, shape, 0, RIGHT_SLOTS)
    result_slot = jax.random.randint(third, shape, 0, TOTAL_SLOTS)
    left_slot = left_slot.at[0, 0, 0, 0, 0].set(LEFT_SLOTS - 1)
    right_slot = right_slot.at[0, 0, 0, 0, 0].set(RIGHT_SLOTS - 1)
    result_slot = result_slot.at[0, 0, 0, 0, 0].set(TOTAL_SLOTS - 1)
    return jnp.stack([left_slot, right_slot, result_slot], axis=4).astype(jnp.int32)


def draw_counts(key, part):
    key = jax.random.fold_in(key, 23)
    first, second, third, fourth = jax.random.split(key, 4)
    devices = GRID_ROWS * GRID_COLS * LAYERS
    level = jnp.minimum(jax.random.randint(first, (devices,), 1, PRODUCTS + 1), jax.random.randint(second, (devices,), 1, PRODUCTS + 1))
    busiest = jax.random.randint(third, (), 0, devices)
    level = level.at[busiest].set(PRODUCTS)
    level = jnp.broadcast_to(level[:, None], (devices, CANNON_STEPS))
    cut = jax.random.randint(fourth, (devices, CANNON_STEPS), 0, level // 4 + 1)
    result = (level - cut).at[busiest, 0].set(PRODUCTS)
    return result.reshape(GRID_ROWS, GRID_COLS, LAYERS, CANNON_STEPS).astype(jnp.int32)


def level_of(key, dims, cuts, smallest, top_value):
    level = 1.0
    for dim, blocks in cuts:
        steps = jax.random.uniform(jax.random.fold_in(jax.random.fold_in(key, 6), dim), (blocks,), jnp.float32, smallest / len(cuts), top_value / len(cuts))
        level = level * jnp.repeat(jnp.exp(steps), dims[dim] // blocks).reshape((-1,) + (1,) * (len(dims) - 1 - dim))
    return level


def gaussian(stream_key, extent, spread, bound, cuts=(), held_as=jnp.bfloat16):
    values = spread * jax.random.normal(stream_key, extent, jnp.float32)
    if cuts:
        values = values * level_of(stream_key, extent, cuts, -0.22, 0.18)
    return jnp.clip(values, -bound, bound).astype(held_as)


def setup_inputs(seed: int = 0) -> dict:
    key_list = jax.random.split(jax.random.key(seed), 6)
    left_tiles = gaussian(key_list[0], (GRID_ROWS, GRID_COLS, LAYERS, LEFT_SLOTS, TILE_EDGE * TILE_EDGE), 0.125, 2.0, ((0, 8), (1, 8), (2, 4)), jnp.float32)
    right_tiles = gaussian(key_list[1], (GRID_ROWS, GRID_COLS, LAYERS, PANEL_QUEUE, RIGHT_SLOTS, TILE_EDGE * TILE_EDGE), 0.125, 2.0, ((0, 8), (1, 8), (2, 4)), jnp.float32)
    square_tiles = gaussian(key_list[2], (GRID_ROWS, GRID_COLS, TOTAL_SLOTS, TILE_EDGE * TILE_EDGE), 0.3, 4.0, ((0, 8), (1, 8), (2, 4)), jnp.float32)
    pairs = draw_pairs(jax.random.fold_in(key_list[5], 71), 0)
    counts = draw_counts(jax.random.fold_in(key_list[5], 71), 0)
    return {"left_tiles": left_tiles, "right_tiles": right_tiles, "square_tiles": square_tiles, "pairs": pairs, "counts": counts}


def contribute(left_panel, right_panel, triple, weight):
    left_tile = jnp.take(left_panel, triple[0], axis=0).reshape(-1, TILE_EDGE, TILE_EDGE)
    right_tile = jnp.take(right_panel, triple[1], axis=0).reshape(-1, TILE_EDGE, TILE_EDGE)
    products = jnp.einsum("pij,pjk->pik", left_tile, right_tile, precision=lax.Precision.HIGHEST)
    products = products.reshape(-1, TILE_EDGE * TILE_EDGE) * weight[:, None]
    return jax.ops.segment_sum(products, triple[2], num_segments=TOTAL_SLOTS)


def reference(left_tiles, right_tiles, square_tiles, pairs, counts):
    active = (jnp.arange(PRODUCTS, dtype=jnp.int32)[None, None, None, None, :] < counts[..., None]).astype(jnp.float32)

    def one_row(grid_row):
        partial_value = jnp.zeros((GRID_COLS, LAYERS, TOTAL_SLOTS, TILE_EDGE * TILE_EDGE), jnp.float32)
        for step_index in range(CANNON_STEPS):
            left_panel = jnp.roll(left_tiles[grid_row], -step_index, axis=0)
            source = ((grid_row + step_index) % GRID_ROWS).astype(jnp.int32)
            queue_slot = (((grid_row + step_index) // GRID_ROWS) % PANEL_QUEUE).astype(jnp.int32)
            right_queue = right_tiles[source]
            right_panel = jnp.take(right_queue, queue_slot, axis=2)
            triple = pairs[grid_row, :, :, step_index]
            weight = active[grid_row, :, :, step_index]
            partial_value = partial_value + jax.vmap(jax.vmap(contribute))(left_panel, right_panel, triple, weight)
        return jnp.sum(partial_value, axis=1)

    product = lax.map(one_row, jnp.arange(GRID_ROWS, dtype=jnp.int32))
    return 3.0 * square_tiles - 2.0 * product
```

```python
import functools

import jax
import jax.numpy as jnp
from jax import lax
from jax.experimental import pallas as pl
from jax.experimental.pallas import tpu as pltpu
from jax.sharding import PartitionSpec as P

AXES = ("row", "col", "depth")
F32 = jnp.float32
BF16 = jnp.bfloat16
TILES = 32
SLOTS = 128
UNROLL = 32


def moved(x, target):
    pairs = []
    for y in range(4):
        for zh in range(2):
            for zl in range(4):
                for c in range(2):
                    for d in range(4):
                        ty, th, tl, tc, td = target(y, zh, zl, c, d)
                        source = ((y * 2 + zh) * 8 + zl * 2 + c) * 4 + d
                        dest = ((ty % 4 * 2 + th % 2) * 8 + tl % 4 * 2 + tc % 2) * 4 + td % 4
                        pairs.append((source, dest))
    return lax.ppermute(x, AXES, pairs)


def by_y(x, k):
    return moved(x, lambda y, zh, zl, c, d: (y + k, zh, zl, c, d))


def by_zl(x, k):
    return moved(x, lambda y, zh, zl, c, d: (y, zh, zl + k, c, d))


def by_depth(x, k):
    return moved(x, lambda y, zh, zl, c, d: (y, zh, zl, c, d + k))


def swap_zh(x):
    return moved(x, lambda y, zh, zl, c, d: (y, zh + 1, zl, c, d))


def swap_core(x):
    return moved(x, lambda y, zh, zl, c, d: (y, zh, zl, c + 1, d))


def split(p):
    high = p.astype(BF16).astype(F32)
    return high, p - high


def section_kernel(jobs, n_left, n_right, has_acc, *refs):
    place, pairs, counts = refs[:3]
    lefts = refs[3 : 3 + n_left]
    rights = refs[3 + n_left : 3 + n_left + n_right]
    rest = refs[3 + n_left + n_right :]
    if has_acc:
        start, rest = rest[0], rest[1:]
    out, lbuf, rbuf, a3, b3, sem, acc_sem = rest
    shift, core, depth = place[0], place[1], place[2]
    lane = lax.broadcasted_iota(jnp.int32, (32, 128), 1) < 64

    def section(job):
        k, odd = job[0], job[1]
        return lax.rem(2 * k + 9 - 2 * core, 8) if odd else 2 * k

    def fetch(j):
        k, odd, left, choices = jobs[j]
        slot = j % 2
        pltpu.make_async_copy(lefts[left], lbuf.at[slot], sem.at[slot, 0]).start()
        if len(choices) == 1:
            pltpu.make_async_copy(rights[choices[0][1]], rbuf.at[slot], sem.at[slot, 1]).start()
        else:
            want = lax.rem(k + shift + 4, 4)
            for offset, index in choices:

                @pl.when(want == offset)
                def _():
                    pltpu.make_async_copy(rights[index], rbuf.at[slot], sem.at[slot, 1]).start()

    def wait(j):
        slot = j % 2
        pltpu.make_async_copy(lefts[0], lbuf.at[slot], sem.at[slot, 0]).wait()
        pltpu.make_async_copy(rights[0], rbuf.at[slot], sem.at[slot, 1]).wait()

    fetch(0)
    if has_acc:
        load = pltpu.make_async_copy(start, out, acc_sem.at[0])
        load.start()
    else:
        out[...] = jnp.zeros_like(out)
    for j in range(len(jobs)):
        if j + 1 < len(jobs):
            fetch(j + 1)
        wait(j)
        slot = j % 2

        @pl.loop(0, TILES, unroll=4)
        def _(t):
            h, low = split(lbuf[slot, t])
            hr = pltpu.roll(h, 64, 1)
            lr = pltpu.roll(low, 64, 1)
            a3[t, 0:32, 0:128] = jnp.where(lane, h, hr).astype(BF16)
            a3[t, 32:64, 0:128] = jnp.where(lane, hr, h).astype(BF16)
            a3[t, 0:32, 128:256] = jnp.where(lane, low, lr).astype(BF16)
            a3[t, 32:64, 128:256] = jnp.where(lane, lr, low).astype(BF16)
            h, low = split(rbuf[slot, t])
            hr = pltpu.roll(h, 64, 1)
            lr = pltpu.roll(low, 64, 1)
            parts = (
                jnp.where(lane, h, hr).astype(BF16),
                jnp.where(lane, hr, h).astype(BF16),
                jnp.where(lane, low, lr).astype(BF16),
                jnp.where(lane, lr, low).astype(BF16),
            )
            for base in (0, 128):
                for i in range(4):
                    b3[t, base + 32 * i : base + 32 * i + 32] = parts[i]

        if j == 0 and has_acc:
            load.wait()
        s = section(jobs[j])
        live = counts[s]

        @pl.loop(0, (live + UNROLL - 1) // UNROLL)
        def _(block):
            sums, slots = [], []
            for u in range(UNROLL):
                p = block * UNROLL + u
                c = jnp.dot(a3[pairs[s, 0, p]], b3[pairs[s, 1, p]], preferred_element_type=F32)
                sums.append(jnp.where(lane, c[0:32], c[32:64]))
                g = lax.rem(pairs[s, 2, p] + (4 - depth) * 32, SLOTS)
                slots.append(jnp.where(p < live, g, SLOTS))
            for u in range(UNROLL):
                out[slots[u]] += sums[u]


def add_sections(jobs, place, pattern, limits, lefts, rights, acc, name):
    smem = pl.BlockSpec(memory_space=pltpu.SMEM)
    anywhere = pl.BlockSpec(memory_space=pl.ANY)
    operands = [place, pattern, limits, *lefts, *rights]
    specs = [smem] * 3 + [anywhere] * (len(lefts) + len(rights))
    if acc is not None:
        operands.append(acc)
        specs.append(anywhere)
    n = len(jobs)
    return pl.pallas_call(
        functools.partial(section_kernel, jobs, len(lefts), len(rights), acc is not None),
        out_shape=jax.ShapeDtypeStruct((SLOTS + 1, 32, 128), F32),
        in_specs=specs,
        out_specs=pl.BlockSpec(memory_space=pltpu.VMEM),
        scratch_shapes=[
            pltpu.VMEM((2, TILES, 32, 128), F32),
            pltpu.VMEM((2, TILES, 32, 128), F32),
            pltpu.VMEM((TILES, 64, 256), BF16),
            pltpu.VMEM((TILES, 256, 128), BF16),
            pltpu.SemaphoreType.DMA((2, 2)),
            pltpu.SemaphoreType.DMA((1,)),
        ],
        compiler_params=pltpu.CompilerParams(vmem_limit_bytes=24 << 20),
        cost_estimate=pl.CostEstimate(
            flops=n * 64 * 2 * 64 * 256 * 128, bytes_accessed=n * (1 << 20) + (4 << 20), transcendentals=0
        ),
        name=name,
    )(*operands)


def on_device(left_tiles, right_tiles, square_tiles, pairs, counts):
    row, col = lax.axis_index("row"), lax.axis_index("col")
    core = col % 2
    place = jnp.stack([row % 2 - core, core, lax.axis_index("depth")]).astype(jnp.int32)
    pattern, limits = pairs[0, 0, 0], counts[0, 0, 0]

    right = right_tiles[0, 0, 0, 0].reshape(TILES, 2, 32, 64).transpose(0, 2, 1, 3).reshape(TILES, 32, 128)
    left = left_tiles[0, 0, 0].reshape(TILES, 32, 128)

    other0 = swap_zh(right)
    left1 = by_zl(left, -1)
    same = [right, by_y(right, -1), by_y(right, 2), by_y(right, 1)]
    left2 = by_zl(left1, -1)
    other = [other0, by_y(other0, -1), by_y(other0, 2), by_y(other0, 1)]
    left3 = by_zl(left2, -1)
    mine = [left, left1, left2, left3]
    twin = [swap_core(x) for x in mine]

    choices = [(i, i) for i in range(4)]
    acc = add_sections([(0, False, 0, [(0, 0)]), (1, False, 1, [(1, 1)])], place, pattern, limits, mine[:2], same[:2], None, "first")
    jobs = [(2, False, 3, [(2, 4)])] + [(k, True, k, choices) for k in range(3)]
    acc = add_sections(jobs, place, pattern, limits, twin[:3] + [mine[2]], other + [same[2]], acc, "second")
    jobs = [(3, False, 1, [(3, 4)]), (3, True, 0, choices)]
    acc = add_sections(jobs, place, pattern, limits, [twin[3], mine[3]], other + [same[3]], acc, "third")

    share = acc[0:32]
    for k in range(1, 4):
        share = share + by_depth(acc[32 * k : 32 * k + 32], k)
    purified = 3.0 * square_tiles[0, 0] - 2.0 * share.reshape(TILES, 4096)
    return purified[None, None]


def solution(mesh):
    in_specs = (
        P("row", "col", "depth", None, None),
        P("row", "col", "depth", None, None, None),
        P("row", "col", "depth", None),
        P("row", "col", "depth", None, None, None),
        P("row", "col", "depth", None),
    )
    out_specs = P("row", "col", "depth", None)
    return jax.shard_map(
        on_device, mesh=mesh, in_specs=in_specs, out_specs=out_specs, check_vma=False
    )
```

```python
import functools

import jax
import jax.numpy as jnp
from jax import lax
from jax.experimental import pallas as pl
from jax.experimental.pallas import tpu as pltpu
from jax.sharding import PartitionSpec as P

AXES = ("row", "col", "depth")
F32 = jnp.float32
BF16 = jnp.bfloat16
TILES = 32
SLOTS = 128
UNROLL = 32


def moved(x, target):
    pairs = []
    for y in range(4):
        for zh in range(2):
            for zl in range(4):
                for c in range(2):
                    for d in range(4):
                        ty, th, tl, tc, td = target(y, zh, zl, c, d)
                        source = ((y * 2 + zh) * 8 + zl * 2 + c) * 4 + d
                        dest = ((ty % 4 * 2 + th % 2) * 8 + tl % 4 * 2 + tc % 2) * 4 + td % 4
                        pairs.append((source, dest))
    return lax.ppermute(x, AXES, pairs)


def by_y(x, k):
    return moved(x, lambda y, zh, zl, c, d: (y + k, zh, zl, c, d))


def by_zl(x, k):
    return moved(x, lambda y, zh, zl, c, d: (y, zh, zl + k, c, d))


def by_depth(x, k):
    return moved(x, lambda y, zh, zl, c, d: (y, zh, zl, c, d + k))


def swap_zh(x):
    return moved(x, lambda y, zh, zl, c, d: (y, zh + 1, zl, c, d))


def swap_core(x):
    return moved(x, lambda y, zh, zl, c, d: (y, zh, zl, c + 1, d))


def split(p):
    high = p.astype(BF16).astype(F32)
    return high, p - high


def section_kernel(jobs, n_left, n_right, has_acc, *refs):
    place, pairs, counts = refs[:3]
    lefts = refs[3 : 3 + n_left]
    rights = refs[3 + n_left : 3 + n_left + n_right]
    rest = refs[3 + n_left + n_right :]
    if has_acc:
        start, rest = rest[0], rest[1:]
    out, lbuf, rbuf, rows, a3, b3, sem, acc_sem = rest
    shift, core, depth = place[0], place[1], place[2]
    lane = lax.broadcasted_iota(jnp.int32, (32, 128), 1) < 64

    def section(job):
        k, odd = job[0], job[1]
        return lax.rem(2 * k + 9 - 2 * core, 8) if odd else 2 * k

    def fetch(j):
        k, odd, left, choices = jobs[j]
        slot = j % 2
        pltpu.make_async_copy(lefts[left], lbuf.at[slot], sem.at[slot, 0]).start()
        if len(choices) == 1:
            pltpu.make_async_copy(rights[choices[0][1]], rbuf.at[slot], sem.at[slot, 1]).start()
        else:
            want = lax.rem(k + shift + 4, 4)
            for offset, index in choices:

                @pl.when(want == offset)
                def _():
                    pltpu.make_async_copy(rights[index], rbuf.at[slot], sem.at[slot, 1]).start()

    def wait(j):
        slot = j % 2
        pltpu.make_async_copy(lefts[0], lbuf.at[slot], sem.at[slot, 0]).wait()
        pltpu.make_async_copy(rights[0], rbuf.at[slot], sem.at[slot, 1]).wait()

    fetch(0)
    if has_acc:
        load = pltpu.make_async_copy(start, out, acc_sem.at[0])
        load.start()
    else:
        out[...] = jnp.zeros_like(out)
    for j in range(len(jobs)):
        if j + 1 < len(jobs):
            fetch(j + 1)
        wait(j)
        slot = j % 2

        @pl.loop(0, TILES, unroll=4)
        def _(t):
            h, low = split(lbuf[slot, t])
            hr = pltpu.roll(h, 64, 1)
            lr = pltpu.roll(low, 64, 1)
            a3[t, 0:32, 0:128] = jnp.where(lane, h, hr).astype(BF16)
            a3[t, 32:64, 0:128] = jnp.where(lane, hr, h).astype(BF16)
            a3[t, 0:32, 128:256] = jnp.where(lane, low, lr).astype(BF16)
            a3[t, 32:64, 128:256] = jnp.where(lane, lr, low).astype(BF16)
            r = rbuf[slot, t]
            rr = pltpu.roll(r, 64, 1)
            rows[t, pl.ds(0, 32, stride=2)] = jnp.where(lane, r, rr)
            rows[t, pl.ds(1, 32, stride=2)] = jnp.where(lane, rr, r)

        @pl.loop(0, TILES, unroll=4)
        def _(t):
            h, low = split(rows[t])
            h = h.astype(BF16)
            low = low.astype(BF16)
            b3[t, 0:64] = h
            b3[t, 64:128] = low
            b3[t, 128:192] = h
            b3[t, 192:256] = low

        if j == 0 and has_acc:
            load.wait()
        s = section(jobs[j])
        live = counts[s]

        @pl.loop(0, (live + UNROLL - 1) // UNROLL)
        def _(block):
            sums, slots = [], []
            for u in range(UNROLL):
                p = block * UNROLL + u
                c = jnp.dot(a3[pairs[s, 0, p]], b3[pairs[s, 1, p]], preferred_element_type=F32)
                sums.append(jnp.where(lane, c[0:32], c[32:64]))
                g = lax.rem(pairs[s, 2, p] + (4 - depth) * 32, SLOTS)
                slots.append(jnp.where(p < live, g, SLOTS))
            for u in range(UNROLL):
                out[slots[u]] += sums[u]


def add_sections(jobs, place, pattern, limits, lefts, rights, acc, name, weight=1):
    smem = pl.BlockSpec(memory_space=pltpu.SMEM)
    anywhere = pl.BlockSpec(memory_space=pl.ANY)
    operands = [place, pattern, limits, *lefts, *rights]
    specs = [smem] * 3 + [anywhere] * (len(lefts) + len(rights))
    if acc is not None:
        operands.append(acc)
        specs.append(anywhere)
    n = len(jobs)
    return pl.pallas_call(
        functools.partial(section_kernel, jobs, len(lefts), len(rights), acc is not None),
        out_shape=jax.ShapeDtypeStruct((SLOTS + 1, 32, 128), F32),
        in_specs=specs,
        out_specs=pl.BlockSpec(memory_space=pltpu.VMEM),
        scratch_shapes=[
            pltpu.VMEM((2, TILES, 32, 128), F32),
            pltpu.VMEM((2, TILES, 32, 128), F32),
            pltpu.VMEM((TILES, 64, 128), F32),
            pltpu.VMEM((TILES, 64, 256), BF16),
            pltpu.VMEM((TILES, 256, 128), BF16),
            pltpu.SemaphoreType.DMA((2, 2)),
            pltpu.SemaphoreType.DMA((1,)),
        ],
        compiler_params=pltpu.CompilerParams(vmem_limit_bytes=24 << 20),
        cost_estimate=pl.CostEstimate(
            flops=weight * n * 64 * 2 * 64 * 256 * 128, bytes_accessed=n * (1 << 20) + (4 << 20), transcendentals=0
        ),
        name=name,
    )(*operands)


def reduce_over_depth(acc):
    up = by_depth(acc[48:80], 1)
    down = by_depth(acc[80:112], -1)
    up2 = by_depth(acc[32:48] + up[16:32], 1)
    down2 = by_depth(acc[112:128] + down[0:16], -1)
    return jnp.concatenate([acc[0:16] + down[16:32] + up2, acc[16:32] + up[0:16] + down2])


def on_device(left_tiles, right_tiles, square_tiles, pairs, counts):
    row, col = lax.axis_index("row"), lax.axis_index("col")
    core = col % 2
    place = jnp.stack([row % 2 - core, core, lax.axis_index("depth")]).astype(jnp.int32)
    pattern, limits = pairs[0, 0, 0], counts[0, 0, 0]

    right = right_tiles[0, 0, 0, 0].reshape(TILES, 32, 128)
    left = left_tiles[0, 0, 0].reshape(TILES, 32, 128)

    args = (place, pattern, limits)
    choices = [(i, i) for i in range(4)]
    other0 = swap_zh(right)
    left1 = by_zl(left, -1)
    same1, same3, same2 = by_y(right, -1), by_y(right, 1), by_y(right, 2)
    left2 = by_zl(left1, -1)
    twin0 = swap_core(left)
    jobs = [(0, False, 0, [(0, 0)]), (1, False, 1, [(1, 1)])]
    acc = add_sections(jobs, *args, [left, left1], [right, same1], None, "first")
    other0, acc, same2, same3 = lax.optimization_barrier((other0, acc, same2, same3))

    other1, other3, other2 = by_y(other0, -1), by_y(other0, 1), by_y(other0, 2)
    left3 = by_zl(left2, -1)
    twin1 = swap_core(left1)
    twin2 = swap_core(left2)
    acc = add_sections([(2, False, 0, [(2, 0)])], *args, [left2], [same2], acc, "second")

    other = [other0, other1, other2, other3]
    jobs = [(k, True, k, choices) for k in range(3)]
    acc = add_sections(jobs, *args, [twin0, twin1, twin2], other, acc, "third")

    left3, acc = lax.optimization_barrier((left3, acc))
    twin3 = swap_core(left3)
    jobs = [(3, False, 1, [(3, 4)]), (3, True, 0, choices)]
    acc = add_sections(jobs, *args, [twin3, left3], other + [same3], acc, "fourth")
    share = reduce_over_depth(acc)
    purified = 3.0 * square_tiles[0, 0] - 2.0 * share.reshape(TILES, 4096)
    return purified[None, None]


def solution(mesh):
    in_specs = (
        P("row", "col", "depth", None, None),
        P("row", "col", "depth", None, None, None),
        P("row", "col", "depth", None),
        P("row", "col", "depth", None, None, None),
        P("row", "col", "depth", None),
    )
    out_specs = P("row", "col", "depth", None)
    return jax.shard_map(
        on_device, mesh=mesh, in_specs=in_specs, out_specs=out_specs, check_vma=False
    )
```

```python
import functools

import jax
import jax.numpy as jnp
from jax import lax
from jax.experimental import pallas as pl
from jax.experimental.pallas import tpu as pltpu
from jax.sharding import PartitionSpec as P

AXES = ("row", "col", "depth")
F32 = jnp.float32
BF16 = jnp.bfloat16
TILES = 32
SLOTS = 128
UNROLL = 32


def moved(x, target):
    pairs = []
    for y in range(4):
        for zh in range(2):
            for zl in range(4):
                for c in range(2):
                    for d in range(4):
                        ty, th, tl, tc, td = target(y, zh, zl, c, d)
                        source = ((y * 2 + zh) * 8 + zl * 2 + c) * 4 + d
                        dest = ((ty % 4 * 2 + th % 2) * 8 + tl % 4 * 2 + tc % 2) * 4 + td % 4
                        pairs.append((source, dest))
    return lax.ppermute(x, AXES, pairs)


def by_y(x, k):
    return moved(x, lambda y, zh, zl, c, d: (y + k, zh, zl, c, d))


def by_zl(x, k):
    return moved(x, lambda y, zh, zl, c, d: (y, zh, zl + k, c, d))


def by_depth(x, k):
    return moved(x, lambda y, zh, zl, c, d: (y, zh, zl, c, d + k))


def swap_zh(x):
    return moved(x, lambda y, zh, zl, c, d: (y, zh + 1, zl, c, d))


def swap_core(x):
    return moved(x, lambda y, zh, zl, c, d: (y, zh, zl, c + 1, d))


def split(p):
    high = p.astype(BF16).astype(F32)
    return high, p - high


def section_kernel(jobs, n_left, n_right, has_acc, *refs):
    place, pairs, counts = refs[:3]
    lefts = refs[3 : 3 + n_left]
    rights = refs[3 + n_left : 3 + n_left + n_right]
    rest = refs[3 + n_left + n_right :]
    if has_acc:
        start, rest = rest[0], rest[1:]
    out, lbuf, rbuf, rows, a3, b3, sem, acc_sem = rest
    shift, core, depth = place[0], place[1], place[2]
    lane = lax.broadcasted_iota(jnp.int32, (32, 128), 1) < 64

    def section(job):
        k, odd = job[0], job[1]
        return lax.rem(2 * k + 9 - 2 * core, 8) if odd else 2 * k

    def fetch(j):
        k, odd, left, choices = jobs[j]
        slot = j % 2
        pltpu.make_async_copy(lefts[left], lbuf.at[slot], sem.at[slot, 0]).start()
        if len(choices) == 1:
            pltpu.make_async_copy(rights[choices[0][1]], rbuf.at[slot], sem.at[slot, 1]).start()
        else:
            want = lax.rem(k + shift + 4, 4)
            for offset, index in choices:

                @pl.when(want == offset)
                def _():
                    pltpu.make_async_copy(rights[index], rbuf.at[slot], sem.at[slot, 1]).start()

    def wait(j):
        slot = j % 2
        pltpu.make_async_copy(lefts[0], lbuf.at[slot], sem.at[slot, 0]).wait()
        pltpu.make_async_copy(rights[0], rbuf.at[slot], sem.at[slot, 1]).wait()

    fetch(0)
    if has_acc:
        load = pltpu.make_async_copy(start, out, acc_sem.at[0])
        load.start()
    else:
        out[...] = jnp.zeros_like(out)
    for j in range(len(jobs)):
        if j + 1 < len(jobs):
            fetch(j + 1)
        wait(j)
        slot = j % 2

        @pl.loop(0, TILES, unroll=4)
        def _(t):
            h, low = split(lbuf[slot, t])
            hr = pltpu.roll(h, 64, 1)
            lr = pltpu.roll(low, 64, 1)
            a3[t, 0:32, 0:128] = jnp.where(lane, h, hr).astype(BF16)
            a3[t, 32:64, 0:128] = jnp.where(lane, hr, h).astype(BF16)
            a3[t, 0:32, 128:256] = jnp.where(lane, low, lr).astype(BF16)
            a3[t, 32:64, 128:256] = jnp.where(lane, lr, low).astype(BF16)
            r = rbuf[slot, t]
            rr = pltpu.roll(r, 64, 1)
            rows[t, pl.ds(0, 32, stride=2)] = jnp.where(lane, r, rr)
            rows[t, pl.ds(1, 32, stride=2)] = jnp.where(lane, rr, r)

        @pl.loop(0, TILES, unroll=4)
        def _(t):
            h, low = split(rows[t])
            h = h.astype(BF16)
            low = low.astype(BF16)
            b3[t, 0:64] = h
            b3[t, 64:128] = low
            b3[t, 128:192] = h
            b3[t, 192:256] = low

        if j == 0 and has_acc:
            load.wait()
        s = section(jobs[j])
        live = counts[s]

        @pl.loop(0, (live + UNROLL - 1) // UNROLL)
        def _(block):
            sums, slots = [], []
            for u in range(UNROLL):
                p = block * UNROLL + u
                c = jnp.dot(a3[pairs[s, 0, p]], b3[pairs[s, 1, p]], preferred_element_type=F32)
                sums.append(jnp.where(lane, c[0:32], c[32:64]))
                g = lax.rem(pairs[s, 2, p] + (4 - depth) * 32, SLOTS)
                slots.append(jnp.where(p < live, g, SLOTS))
            for u in range(UNROLL):
                out[slots[u]] += sums[u]


def add_sections(jobs, place, pattern, limits, lefts, rights, acc, name):
    smem = pl.BlockSpec(memory_space=pltpu.SMEM)
    anywhere = pl.BlockSpec(memory_space=pl.ANY)
    operands = [place, pattern, limits, *lefts, *rights]
    specs = [smem] * 3 + [anywhere] * (len(lefts) + len(rights))
    if acc is not None:
        operands.append(acc)
        specs.append(anywhere)
    return pl.pallas_call(
        functools.partial(section_kernel, jobs, len(lefts), len(rights), acc is not None),
        out_shape=jax.ShapeDtypeStruct((SLOTS + 1, 32, 128), F32),
        in_specs=specs,
        out_specs=pl.BlockSpec(memory_space=pltpu.VMEM),
        scratch_shapes=[
            pltpu.VMEM((2, TILES, 32, 128), F32),
            pltpu.VMEM((2, TILES, 32, 128), F32),
            pltpu.VMEM((TILES, 64, 128), F32),
            pltpu.VMEM((TILES, 64, 256), BF16),
            pltpu.VMEM((TILES, 256, 128), BF16),
            pltpu.SemaphoreType.DMA((2, 2)),
            pltpu.SemaphoreType.DMA((1,)),
        ],
        compiler_params=pltpu.CompilerParams(vmem_limit_bytes=24 << 20),
        cost_estimate=pl.CostEstimate(flops=0, bytes_accessed=0, transcendentals=0),
        name=name,
    )(*operands)


def reduce_over_depth(acc):
    up = by_depth(acc[48:80], 1)
    down = by_depth(acc[80:112], -1)
    up, down = lax.optimization_barrier((up, down))
    up2 = by_depth(acc[32:48] + up[16:32], 1)
    down2 = by_depth(acc[112:128] + down[0:16], -1)
    up2, down2 = lax.optimization_barrier((up2, down2))
    return jnp.concatenate([acc[0:16] + down[16:32] + up2, acc[16:32] + up[0:16] + down2])


def on_device(left_tiles, right_tiles, square_tiles, pairs, counts):
    row, col = lax.axis_index("row"), lax.axis_index("col")
    core = col % 2
    place = jnp.stack([row % 2 - core, core, lax.axis_index("depth")]).astype(jnp.int32)
    pattern, limits = pairs[0, 0, 0], counts[0, 0, 0]

    right = right_tiles[0, 0, 0, 0].reshape(TILES, 32, 128)
    left = left_tiles[0, 0, 0].reshape(TILES, 32, 128)

    args = (place, pattern, limits)
    choices = [(i, i) for i in range(4)]
    other0 = swap_zh(right)
    same1, same3, same2 = by_y(right, -1), by_y(right, 1), by_y(right, 2)
    twin0 = swap_core(left)
    acc = add_sections([(0, False, 0, [(0, 0)])], *args, [left], [right], None, "sections_a")
    same1, acc, left_now = lax.optimization_barrier((same1, acc, left))
    left1 = by_zl(left_now, -1)
    other0, same1, same3, same2, acc = lax.optimization_barrier((other0, same1, same3, same2, acc))

    other1, other3, other2 = by_y(other0, -1), by_y(other0, 1), by_y(other0, 2)
    left2 = by_zl(left1, -1)
    twin1 = swap_core(left1)
    acc = add_sections([(1, False, 0, [(1, 0)])], *args, [left1], [same1], acc, "sections_b")
    left3 = by_zl(left2, -1)
    twin2 = swap_core(left2)
    acc = add_sections([(2, False, 0, [(2, 0)])], *args, [left2], [same2], acc, "sections_c")

    other = [other0, other1, other2, other3]
    jobs = [(k, True, k, choices) for k in range(3)]
    acc = add_sections(jobs, *args, [twin0, twin1, twin2], other, acc, "sections_d")

    left3, acc = lax.optimization_barrier((left3, acc))
    twin3 = swap_core(left3)
    jobs = [(3, False, 1, [(3, 4)]), (3, True, 0, choices)]
    acc = add_sections(jobs, *args, [twin3, left3], other + [same3], acc, "sections_e")
    share = reduce_over_depth(acc)
    purified = 3.0 * square_tiles[0, 0] - 2.0 * share.reshape(TILES, 4096)
    return purified[None, None]


def solution(mesh):
    in_specs = (
        P("row", "col", "depth", None, None),
        P("row", "col", "depth", None, None, None),
        P("row", "col", "depth", None),
        P("row", "col", "depth", None, None, None),
        P("row", "col", "depth", None),
    )
    out_specs = P("row", "col", "depth", None)
    return jax.shard_map(
        on_device, mesh=mesh, in_specs=in_specs, out_specs=out_specs, check_vma=False
    )
```

```python
import functools

import jax
import jax.numpy as jnp
from jax import lax
from jax.experimental import pallas as pl
from jax.experimental.pallas import tpu as pltpu
from jax.sharding import PartitionSpec as P

AXES = ("row", "col", "depth")
F32 = jnp.float32
BF16 = jnp.bfloat16
TILES = 32
SLOTS = 128
UNROLL = 32
PARTS = ((0, 32), (32, 48), (48, 80), (80, 112), (112, 128))


def moved(x, target):
    pairs = []
    for y in range(4):
        for zh in range(2):
            for zl in range(4):
                for c in range(2):
                    for d in range(4):
                        ty, th, tl, tc, td = target(y, zh, zl, c, d)
                        source = ((y * 2 + zh) * 8 + zl * 2 + c) * 4 + d
                        dest = ((ty % 4 * 2 + th % 2) * 8 + tl % 4 * 2 + tc % 2) * 4 + td % 4
                        pairs.append((source, dest))
    return lax.ppermute(x, AXES, pairs)


def by_y(x, k):
    return moved(x, lambda y, zh, zl, c, d: (y + k, zh, zl, c, d))


def by_zl(x, k):
    return moved(x, lambda y, zh, zl, c, d: (y, zh, zl + k, c, d))


def by_depth(x, k):
    return moved(x, lambda y, zh, zl, c, d: (y, zh, zl, c, d + k))


def swap_zh(x):
    return moved(x, lambda y, zh, zl, c, d: (y, zh + 1, zl, c, d))


def swap_core(x):
    return moved(x, lambda y, zh, zl, c, d: (y, zh, zl, c + 1, d))


def split(p):
    high = p.astype(BF16).astype(F32)
    return high, p - high


def section_kernel(jobs, n_left, n_right, has_acc, half, *refs):
    place, pairs, counts = refs[:3]
    lefts = refs[3 : 3 + n_left]
    rights = refs[3 + n_left : 3 + n_left + n_right]
    rest = refs[3 + n_left + n_right :]
    if has_acc:
        start, rest = rest[0], rest[1:]
    if half is None:
        outs, (out, lbuf, rbuf, rows, a3, b3, sem, acc_sem) = (), rest
    else:
        outs, (lbuf, rbuf, rows, a3, b3, sem, acc_sem, out) = rest[:5], rest[5:]
    shift, core, depth = place[0], place[1], place[2]
    lane = lax.broadcasted_iota(jnp.int32, (32, 128), 1) < 64
    height = out.shape[1]
    lane_left = lane[:height]

    def section(job):
        k, odd = job[0], job[1]
        return lax.rem(2 * k + 9 - 2 * core, 8) if odd else 2 * k

    def own_rows(ref):
        return ref if half is None else ref.at[:, pl.ds(height * half, height)]

    def fetch(j):
        k, odd, left, choices = jobs[j]
        slot = j % 2
        pltpu.make_async_copy(own_rows(lefts[left]), lbuf.at[slot], sem.at[slot, 0]).start()
        if len(choices) == 1:
            pltpu.make_async_copy(rights[choices[0][1]], rbuf.at[slot], sem.at[slot, 1]).start()
        else:
            want = lax.rem(k + shift + 4, 4)
            for offset, index in choices:

                @pl.when(want == offset)
                def _():
                    pltpu.make_async_copy(rights[index], rbuf.at[slot], sem.at[slot, 1]).start()

    def wait(j):
        slot = j % 2
        pltpu.make_async_copy(own_rows(lefts[0]), lbuf.at[slot], sem.at[slot, 0]).wait()
        pltpu.make_async_copy(rights[0], rbuf.at[slot], sem.at[slot, 1]).wait()

    fetch(0)
    if has_acc:
        load = pltpu.make_async_copy(own_rows(start), out, acc_sem.at[0])
        load.start()
    else:
        out[...] = jnp.zeros_like(out)
    for j in range(len(jobs)):
        if j + 1 < len(jobs):
            fetch(j + 1)
        wait(j)
        slot = j % 2

        @pl.loop(0, TILES, unroll=4)
        def _(t):
            h, low = split(lbuf[slot, t])
            hr = pltpu.roll(h, 64, 1)
            lr = pltpu.roll(low, 64, 1)
            a3[t, 0:height, 0:128] = jnp.where(lane_left, h, hr).astype(BF16)
            a3[t, height : 2 * height, 0:128] = jnp.where(lane_left, hr, h).astype(BF16)
            a3[t, 0:height, 128:256] = jnp.where(lane_left, low, lr).astype(BF16)
            a3[t, height : 2 * height, 128:256] = jnp.where(lane_left, lr, low).astype(BF16)
            r = rbuf[slot, t]
            rr = pltpu.roll(r, 64, 1)
            rows[t, pl.ds(0, 32, stride=2)] = jnp.where(lane, r, rr)
            rows[t, pl.ds(1, 32, stride=2)] = jnp.where(lane, rr, r)

        @pl.loop(0, TILES, unroll=4)
        def _(t):
            h, low = split(rows[t])
            h = h.astype(BF16)
            low = low.astype(BF16)
            b3[t, 0:64] = h
            b3[t, 64:128] = low
            b3[t, 128:192] = h
            b3[t, 192:256] = low

        if j == 0 and has_acc:
            load.wait()
        s = section(jobs[j])
        live = counts[s]

        @pl.loop(0, (live + UNROLL - 1) // UNROLL)
        def _(block):
            sums, slots = [], []
            for u in range(UNROLL):
                p = block * UNROLL + u
                c = jnp.dot(a3[pairs[s, 0, p]], b3[pairs[s, 1, p]], preferred_element_type=F32)
                sums.append(jnp.where(lane_left, c[0:height], c[height : 2 * height]))
                g = lax.rem(pairs[s, 2, p] + (4 - depth) * 32, SLOTS)
                slots.append(jnp.where(p < live, g, SLOTS))
            for u in range(UNROLL):
                out[slots[u]] += sums[u]

    for ref, (first, last) in zip(outs, PARTS):
        ref[...] = out[first:last]


def add_sections(jobs, place, pattern, limits, lefts, rights, acc, name, half=None):
    smem = pl.BlockSpec(memory_space=pltpu.SMEM)
    anywhere = pl.BlockSpec(memory_space=pl.ANY)
    operands = [place, pattern, limits, *lefts, *rights]
    specs = [smem] * 3 + [anywhere] * (len(lefts) + len(rights))
    if acc is not None:
        operands.append(acc)
        specs.append(anywhere)
    height = 32 if half is None else 16
    vmem = pl.BlockSpec(memory_space=pltpu.VMEM)
    shape = jax.ShapeDtypeStruct((SLOTS + 1, height, 128), F32)
    scratch = []
    if half is not None:
        shape = [jax.ShapeDtypeStruct((last - first, height, 128), F32) for first, last in PARTS]
        scratch = [pltpu.VMEM((SLOTS + 1, height, 128), F32)]
    return pl.pallas_call(
        functools.partial(section_kernel, jobs, len(lefts), len(rights), acc is not None, half),
        out_shape=shape,
        in_specs=specs,
        out_specs=vmem if half is None else [vmem] * len(PARTS),
        scratch_shapes=[
            pltpu.VMEM((2, TILES, height, 128), F32),
            pltpu.VMEM((2, TILES, 32, 128), F32),
            pltpu.VMEM((TILES, 64, 128), F32),
            pltpu.VMEM((TILES, 2 * height, 256), BF16),
            pltpu.VMEM((TILES, 256, 128), BF16),
            pltpu.SemaphoreType.DMA((2, 2)),
            pltpu.SemaphoreType.DMA((1,)),
        ]
        + scratch,
        compiler_params=pltpu.CompilerParams(vmem_limit_bytes=24 << 20),
        cost_estimate=pl.CostEstimate(flops=0, bytes_accessed=0, transcendentals=0),
        name=name,
    )(*operands)


def reduce_over_depth(parts):
    own, low, up, down, high = parts
    up, down = by_depth(up, 1), by_depth(down, -1)
    up, down = lax.optimization_barrier((up, down))
    up2 = by_depth(low + up[16:32], 1)
    down2 = by_depth(high + down[0:16], -1)
    up2, down2 = lax.optimization_barrier((up2, down2))
    return jnp.concatenate([own[0:16] + down[16:32] + up2, own[16:32] + up[0:16] + down2])


def on_device(left_tiles, right_tiles, square_tiles, pairs, counts):
    row, col = lax.axis_index("row"), lax.axis_index("col")
    core = col % 2
    place = jnp.stack([row % 2 - core, core, lax.axis_index("depth")]).astype(jnp.int32)
    pattern, limits = pairs[0, 0, 0], counts[0, 0, 0]

    right = right_tiles[0, 0, 0, 0].reshape(TILES, 32, 128)
    left = left_tiles[0, 0, 0].reshape(TILES, 32, 128)

    args = (place, pattern, limits)
    choices = [(i, i) for i in range(4)]
    other0 = swap_zh(right)
    same1, same3, same2 = by_y(right, -1), by_y(right, 1), by_y(right, 2)
    twin0 = swap_core(left)
    acc = add_sections([(0, False, 0, [(0, 0)])], *args, [left], [right], None, "sections_a")
    same1, acc, left_now = lax.optimization_barrier((same1, acc, left))
    left1 = by_zl(left_now, -1)
    other0, same1, same3, same2, acc = lax.optimization_barrier((other0, same1, same3, same2, acc))

    other1, other3, other2 = by_y(other0, -1), by_y(other0, 1), by_y(other0, 2)
    left2 = by_zl(left1, -1)
    twin1 = swap_core(left1)
    acc = add_sections([(1, False, 0, [(1, 0)])], *args, [left1], [same1], acc, "sections_b")
    left2, other1, other3, other2, acc = lax.optimization_barrier((left2, other1, other3, other2, acc))

    left3 = by_zl(left2, -1)
    twin2 = swap_core(left2)
    other = [other0, other1, other2, other3]
    jobs = [(2, False, 0, [(2, 4)])] + [(k, True, k + 1, choices) for k in range(3)]
    acc = add_sections(jobs, *args, [left2, twin0, twin1, twin2], other + [same2], acc, "sections_c")

    jobs = [(3, False, 1, [(3, 4)]), (3, True, 0, choices)]
    left3, acc = lax.optimization_barrier((left3, acc))
    twin3 = swap_core(left3)
    share = [
        add_sections(jobs, *args, [twin3, left3], other + [same3], acc, f"sections_e{h}", h) for h in range(2)
    ]
    share = [reduce_over_depth(half) for half in share]
    share = jnp.concatenate(share, axis=1)
    purified = 3.0 * square_tiles[0, 0] - 2.0 * share.reshape(TILES, 4096)
    return purified[None, None]


def solution(mesh):
    in_specs = (
        P("row", "col", "depth", None, None),
        P("row", "col", "depth", None, None, None),
        P("row", "col", "depth", None),
        P("row", "col", "depth", None, None, None),
        P("row", "col", "depth", None),
    )
    out_specs = P("row", "col", "depth", None)
    return jax.shard_map(
        on_device, mesh=mesh, in_specs=in_specs, out_specs=out_specs, check_vma=False
    )
```

```python
import functools

import jax
import jax.numpy as jnp
from jax import lax
from jax.experimental import pallas as pl
from jax.experimental.pallas import tpu as pltpu
from jax.sharding import PartitionSpec as P

AXES = ("row", "col", "depth")
F32 = jnp.float32
BF16 = jnp.bfloat16
TILES = 32
SLOTS = 128
UNROLL = 32
PARTS = ((0, 32), (32, 48), (48, 80), (80, 112), (112, 128))


def moved(x, target):
    pairs = []
    for y in range(4):
        for zh in range(2):
            for zl in range(4):
                for c in range(2):
                    for d in range(4):
                        ty, th, tl, tc, td = target(y, zh, zl, c, d)
                        source = ((y * 2 + zh) * 8 + zl * 2 + c) * 4 + d
                        dest = ((ty % 4 * 2 + th % 2) * 8 + tl % 4 * 2 + tc % 2) * 4 + td % 4
                        pairs.append((source, dest))
    return lax.ppermute(x, AXES, pairs)


def by_y(x, k):
    return moved(x, lambda y, zh, zl, c, d: (y + k, zh, zl, c, d))


def by_zl(x, k):
    return moved(x, lambda y, zh, zl, c, d: (y, zh, zl + k, c, d))


def by_depth(x, k):
    return moved(x, lambda y, zh, zl, c, d: (y, zh, zl, c, d + k))


def swap_zh(x):
    return moved(x, lambda y, zh, zl, c, d: (y, zh + 1, zl, c, d))


def swap_core(x):
    return moved(x, lambda y, zh, zl, c, d: (y, zh, zl, c + 1, d))


def split(p):
    high = p.astype(BF16).astype(F32)
    return high, p - high


def section_kernel(jobs, n_left, n_right, has_acc, half, *refs):
    place, pairs, counts = refs[:3]
    lefts = refs[3 : 3 + n_left]
    rights = refs[3 + n_left : 3 + n_left + n_right]
    rest = refs[3 + n_left + n_right :]
    if has_acc:
        start, rest = rest[0], rest[1:]
    if half is None:
        outs, (out, lbuf, rbuf, rows, a3, b3, sem, acc_sem) = (), rest
    else:
        outs, (lbuf, rbuf, rows, a3, b3, sem, acc_sem, out) = rest[:5], rest[5:]
    shift, core, depth = place[0], place[1], place[2]
    lane = lax.broadcasted_iota(jnp.int32, (32, 128), 1) < 64
    height = out.shape[1]
    lane_left = lane[:height]

    def section(job):
        k, odd = job[0], job[1]
        return lax.rem(2 * k + 9 - 2 * core, 8) if odd else 2 * k

    def own_rows(ref):
        return ref if half is None else ref.at[:, pl.ds(height * half, height)]

    def fetch(j):
        k, odd, left, choices = jobs[j]
        slot = j % 2
        pltpu.make_async_copy(own_rows(lefts[left]), lbuf.at[slot], sem.at[slot, 0]).start()
        if len(choices) == 1:
            pltpu.make_async_copy(rights[choices[0][1]], rbuf.at[slot], sem.at[slot, 1]).start()
        else:
            want = lax.rem(k + shift + 4, 4)
            for offset, index in choices:

                @pl.when(want == offset)
                def _():
                    pltpu.make_async_copy(rights[index], rbuf.at[slot], sem.at[slot, 1]).start()

    def wait(j):
        slot = j % 2
        pltpu.make_async_copy(own_rows(lefts[0]), lbuf.at[slot], sem.at[slot, 0]).wait()
        pltpu.make_async_copy(rights[0], rbuf.at[slot], sem.at[slot, 1]).wait()

    fetch(0)
    if has_acc:
        load = pltpu.make_async_copy(own_rows(start), out, acc_sem.at[0])
        load.start()
    else:
        out[...] = jnp.zeros_like(out)
    for j in range(len(jobs)):
        if j + 1 < len(jobs):
            fetch(j + 1)
        wait(j)
        slot = j % 2

        @pl.loop(0, TILES, unroll=4)
        def _(t):
            h, low = split(lbuf[slot, t])
            hr = pltpu.roll(h, 64, 1)
            lr = pltpu.roll(low, 64, 1)
            a3[t, 0:height, 0:128] = jnp.where(lane_left, h, hr).astype(BF16)
            a3[t, height : 2 * height, 0:128] = jnp.where(lane_left, hr, h).astype(BF16)
            a3[t, 0:height, 128:256] = jnp.where(lane_left, low, lr).astype(BF16)
            a3[t, height : 2 * height, 128:256] = jnp.where(lane_left, lr, low).astype(BF16)
            r = rbuf[slot, t]
            rr = pltpu.roll(r, 64, 1)
            rows[t, pl.ds(0, 32, stride=2)] = jnp.where(lane, r, rr)
            rows[t, pl.ds(1, 32, stride=2)] = jnp.where(lane, rr, r)

        @pl.loop(0, TILES, unroll=4)
        def _(t):
            h, low = split(rows[t])
            h = h.astype(BF16)
            low = low.astype(BF16)
            b3[t, 0:64] = h
            b3[t, 64:128] = low
            b3[t, 128:192] = h
            b3[t, 192:256] = low

        if j == 0 and has_acc:
            load.wait()
        s = section(jobs[j])
        live = counts[s]

        @pl.loop(0, (live + UNROLL - 1) // UNROLL)
        def _(block):
            sums, slots = [], []
            for u in range(UNROLL):
                p = block * UNROLL + u
                c = jnp.dot(a3[pairs[s, 0, p]], b3[pairs[s, 1, p]], preferred_element_type=F32)
                sums.append(jnp.where(lane_left, c[0:height], c[height : 2 * height]))
                g = lax.rem(pairs[s, 2, p] + (4 - depth) * 32, SLOTS)
                slots.append(jnp.where(p < live, g, SLOTS))
            for u in range(UNROLL):
                out[slots[u]] += sums[u]

    for ref, (first, last) in zip(outs, PARTS):
        ref[...] = out[first:last]


def add_sections(jobs, place, pattern, limits, lefts, rights, acc, name, half=None):
    smem = pl.BlockSpec(memory_space=pltpu.SMEM)
    anywhere = pl.BlockSpec(memory_space=pl.ANY)
    operands = [place, pattern, limits, *lefts, *rights]
    specs = [smem] * 3 + [anywhere] * (len(lefts) + len(rights))
    if acc is not None:
        operands.append(acc)
        specs.append(anywhere)
    height = 32 if half is None else 16
    vmem = pl.BlockSpec(memory_space=pltpu.VMEM)
    shape = jax.ShapeDtypeStruct((SLOTS + 1, height, 128), F32)
    scratch = []
    if half is not None:
        shape = [jax.ShapeDtypeStruct((last - first, height, 128), F32) for first, last in PARTS]
        scratch = [pltpu.VMEM((SLOTS + 1, height, 128), F32)]
    return pl.pallas_call(
        functools.partial(section_kernel, jobs, len(lefts), len(rights), acc is not None, half),
        out_shape=shape,
        in_specs=specs,
        out_specs=vmem if half is None else [vmem] * len(PARTS),
        scratch_shapes=[
            pltpu.VMEM((2, TILES, height, 128), F32),
            pltpu.VMEM((2, TILES, 32, 128), F32),
            pltpu.VMEM((TILES, 64, 128), F32),
            pltpu.VMEM((TILES, 2 * height, 256), BF16),
            pltpu.VMEM((TILES, 256, 128), BF16),
            pltpu.SemaphoreType.DMA((2, 2)),
            pltpu.SemaphoreType.DMA((1,)),
        ]
        + scratch,
        compiler_params=pltpu.CompilerParams(vmem_limit_bytes=24 << 20),
        cost_estimate=pl.CostEstimate(flops=0, bytes_accessed=0, transcendentals=0),
        name=name,
    )(*operands)


def reduce_over_depth(parts):
    own, low, up, down, high = parts
    up, down = by_depth(up, 1), by_depth(down, -1)
    up, down = lax.optimization_barrier((up, down))
    up2 = by_depth(low + up[16:32], 1)
    down2 = by_depth(high + down[0:16], -1)
    up2, down2 = lax.optimization_barrier((up2, down2))
    return jnp.concatenate([own[0:16] + down[16:32] + up2, own[16:32] + up[0:16] + down2])


def on_device(left_tiles, right_tiles, square_tiles, pairs, counts):
    row, col = lax.axis_index("row"), lax.axis_index("col")
    core = col % 2
    place = jnp.stack([row % 2 - core, core, lax.axis_index("depth")]).astype(jnp.int32)
    pattern, limits = pairs[0, 0, 0], counts[0, 0, 0]

    right = right_tiles[0, 0, 0, 0].reshape(TILES, 32, 128)
    left = left_tiles[0, 0, 0].reshape(TILES, 32, 128)

    args = (place, pattern, limits)
    choices = [(i, i) for i in range(4)]
    other0 = swap_zh(right)
    same1, same3, same2 = by_y(right, -1), by_y(right, 1), by_y(right, 2)
    twin0 = swap_core(left)
    acc = add_sections([(0, False, 0, [(0, 0)])], *args, [left], [right], None, "sections_a")
    same1, same3, same2, other0, acc, left_now = lax.optimization_barrier((same1, same3, same2, other0, acc, left))

    left1 = by_zl(left_now, -1)
    other1, other3, other2 = by_y(other0, -1), by_y(other0, 1), by_y(other0, 2)
    left2 = by_zl(left1, -1)
    twin1 = swap_core(left1)
    acc = add_sections([(1, False, 0, [(1, 0)])], *args, [left1], [same1], acc, "sections_b")
    other1, other3, other2, left2, acc = lax.optimization_barrier((other1, other3, other2, left2, acc))

    left3 = by_zl(left2, -1)
    twin2 = swap_core(left2)
    other = [other0, other1, other2, other3]
    jobs = [(2, False, 0, [(2, 4)])] + [(k, True, k + 1, choices) for k in range(3)]
    acc = add_sections(jobs, *args, [left2, twin0, twin1, twin2], other + [same2], acc, "sections_c")

    jobs = [(3, False, 1, [(3, 4)]), (3, True, 0, choices)]
    left3, acc = lax.optimization_barrier((left3, acc))
    twin3 = swap_core(left3)
    share = [
        add_sections(jobs, *args, [twin3, left3], other + [same3], acc, f"sections_e{h}", h) for h in range(2)
    ]
    share = [reduce_over_depth(half) for half in share]
    share = jnp.concatenate(share, axis=1)
    purified = 3.0 * square_tiles[0, 0] - 2.0 * share.reshape(TILES, 4096)
    return purified[None, None]


def solution(mesh):
    in_specs = (
        P("row", "col", "depth", None, None),
        P("row", "col", "depth", None, None, None),
        P("row", "col", "depth", None),
        P("row", "col", "depth", None, None, None),
        P("row", "col", "depth", None),
    )
    out_specs = P("row", "col", "depth", None)
    return jax.shard_map(
        on_device, mesh=mesh, in_specs=in_specs, out_specs=out_specs, check_vma=False
    )
```

```python
import functools

import jax
import jax.numpy as jnp
from jax import lax
from jax.experimental import pallas as pl
from jax.experimental.pallas import tpu as pltpu
from jax.sharding import PartitionSpec as P

AXES = ("row", "col", "depth")
F32 = jnp.float32
BF16 = jnp.bfloat16
TILES = 32
SLOTS = 128
UNROLL = 32
PARTS = ((0, 32), (32, 48), (48, 80), (80, 112), (112, 128))


def moved(x, target):
    pairs = []
    for y in range(4):
        for zh in range(2):
            for zl in range(4):
                for c in range(2):
                    for d in range(4):
                        ty, th, tl, tc, td = target(y, zh, zl, c, d)
                        source = ((y * 2 + zh) * 8 + zl * 2 + c) * 4 + d
                        dest = ((ty % 4 * 2 + th % 2) * 8 + tl % 4 * 2 + tc % 2) * 4 + td % 4
                        pairs.append((source, dest))
    return lax.ppermute(x, AXES, pairs)


def by_y(x, k):
    return moved(x, lambda y, zh, zl, c, d: (y + k, zh, zl, c, d))


def by_zl(x, k):
    return moved(x, lambda y, zh, zl, c, d: (y, zh, zl + k, c, d))


def by_depth(x, k):
    return moved(x, lambda y, zh, zl, c, d: (y, zh, zl, c, d + k))


def swap_zh(x):
    return moved(x, lambda y, zh, zl, c, d: (y, zh + 1, zl, c, d))


def swap_core(x):
    return moved(x, lambda y, zh, zl, c, d: (y, zh, zl, c + 1, d))


def split(p):
    high = p.astype(BF16).astype(F32)
    return high, p - high


def section_kernel(jobs, later, n_left, n_right, has_acc, half, *refs):
    place, pairs, counts = refs[:3]
    lefts = refs[3 : 3 + n_left]
    rights = refs[3 + n_left : 3 + n_left + n_right]
    rest = refs[3 + n_left + n_right :]
    if has_acc:
        start, rest = rest[0], rest[1:]
    outs, prepared = (), None
    if half is None:
        out, rest = rest[0], rest[1:]
        if later:
            made, rest = rest[0], rest[1:]
        lbuf, rbuf, rows, a3, b3, sem, acc_sem = rest
    else:
        prepared, outs, (lbuf, a3, sem, acc_sem, out) = rest[0], rest[1:6], rest[6:]
    shift, core, depth = place[0], place[1], place[2]
    lane = lax.broadcasted_iota(jnp.int32, (32, 128), 1) < 64
    height = out.shape[1]
    lane_left = lane[:height]

    def section(job):
        k, odd = job[0], job[1]
        return lax.rem(2 * k + 9 - 2 * core, 8) if odd else 2 * k

    def own_rows(ref):
        return ref if half is None else ref.at[:, pl.ds(height * half, height)]

    def fetch(j):
        k, odd, left, choices = (jobs + later)[j]
        slot = j % 2
        if j < len(jobs):
            pltpu.make_async_copy(own_rows(lefts[left]), lbuf.at[slot], sem.at[slot, 0]).start()
        if prepared is not None:
            return
        if len(choices) == 1:
            pltpu.make_async_copy(rights[choices[0][1]], rbuf.at[slot], sem.at[slot, 1]).start()
        else:
            want = lax.rem(k + shift + 4, 4)
            for offset, index in choices:

                @pl.when(want == offset)
                def _():
                    pltpu.make_async_copy(rights[index], rbuf.at[slot], sem.at[slot, 1]).start()

    def wait(j):
        slot = j % 2
        if j < len(jobs):
            pltpu.make_async_copy(own_rows(lefts[0]), lbuf.at[slot], sem.at[slot, 0]).wait()
        if prepared is None:
            pltpu.make_async_copy(rights[0], rbuf.at[slot], sem.at[slot, 1]).wait()

    def split_right(slot, target):
        @pl.loop(0, TILES, unroll=4)
        def _(t):
            r = rbuf[slot, t]
            rr = pltpu.roll(r, 64, 1)
            rows[t, pl.ds(0, 32, stride=2)] = jnp.where(lane, r, rr)
            rows[t, pl.ds(1, 32, stride=2)] = jnp.where(lane, rr, r)

        @pl.loop(0, TILES, unroll=4)
        def _(t):
            h, low = split(rows[t])
            h = h.astype(BF16)
            low = low.astype(BF16)
            target[t, 0:64] = h
            target[t, 64:128] = low
            target[t, 128:192] = h
            target[t, 192:256] = low

    fetch(0)
    if has_acc:
        load = pltpu.make_async_copy(own_rows(start), out, acc_sem.at[0])
        load.start()
    else:
        out[...] = jnp.zeros_like(out)
    for j in range(len(jobs)):
        if j + 1 < len(jobs + later):
            fetch(j + 1)
        wait(j)
        slot = j % 2

        @pl.loop(0, TILES, unroll=4)
        def _(t):
            h, low = split(lbuf[slot, t])
            hr = pltpu.roll(h, 64, 1)
            lr = pltpu.roll(low, 64, 1)
            a3[t, 0:height, 0:128] = jnp.where(lane_left, h, hr).astype(BF16)
            a3[t, height : 2 * height, 0:128] = jnp.where(lane_left, hr, h).astype(BF16)
            a3[t, 0:height, 128:256] = jnp.where(lane_left, low, lr).astype(BF16)
            a3[t, height : 2 * height, 128:256] = jnp.where(lane_left, lr, low).astype(BF16)

        if prepared is None:
            weights = b3
            split_right(slot, weights)
        else:
            weights = prepared.at[j]
        if j == 0 and has_acc:
            load.wait()
        s = section(jobs[j])
        live = counts[s]

        @pl.loop(0, (live + UNROLL - 1) // UNROLL)
        def _(block):
            sums, slots = [], []
            for u in range(UNROLL):
                p = block * UNROLL + u
                c = jnp.dot(a3[pairs[s, 0, p]], weights[pairs[s, 1, p]], preferred_element_type=F32)
                sums.append(jnp.where(lane_left, c[0:height], c[height : 2 * height]))
                g = lax.rem(pairs[s, 2, p] + (4 - depth) * 32, SLOTS)
                slots.append(jnp.where(p < live, g, SLOTS))
            for u in range(UNROLL):
                out[slots[u]] += sums[u]

    for i in range(len(later)):
        j = len(jobs) + i
        if j + 1 < len(jobs + later):
            fetch(j + 1)
        wait(j)
        split_right(j % 2, made.at[i])
    for ref, (first, last) in zip(outs, PARTS):
        ref[...] = out[first:last]


def add_sections(jobs, place, pattern, limits, lefts, rights, acc, name, later=[], half=None, prepared=None):
    smem = pl.BlockSpec(memory_space=pltpu.SMEM)
    vmem = pl.BlockSpec(memory_space=pltpu.VMEM)
    anywhere = pl.BlockSpec(memory_space=pl.ANY)
    operands = [place, pattern, limits, *lefts, *rights]
    specs = [smem] * 3 + [anywhere] * (len(lefts) + len(rights))
    if acc is not None:
        operands.append(acc)
        specs.append(anywhere)
    height = 32 if half is None else 16
    scratch = [
        pltpu.VMEM((2, TILES, height, 128), F32),
        pltpu.VMEM((2, TILES, 32, 128), F32),
        pltpu.VMEM((TILES, 64, 128), F32),
        pltpu.VMEM((TILES, 2 * height, 256), BF16),
        pltpu.VMEM((TILES, 256, 128), BF16),
        pltpu.SemaphoreType.DMA((2, 2)),
        pltpu.SemaphoreType.DMA((1,)),
    ]
    shapes = [jax.ShapeDtypeStruct((SLOTS + 1, height, 128), F32)]
    if later:
        shapes.append(jax.ShapeDtypeStruct((len(later), TILES, 256, 128), BF16))
    if half is not None:
        operands.append(prepared)
        specs.append(vmem)
        shapes = [jax.ShapeDtypeStruct((last - first, height, 128), F32) for first, last in PARTS]
        scratch = [scratch[0], scratch[3], *scratch[5:], pltpu.VMEM((SLOTS + 1, height, 128), F32)]
    out = pl.pallas_call(
        functools.partial(section_kernel, jobs, later, len(lefts), len(rights), acc is not None, half),
        out_shape=shapes,
        in_specs=specs,
        out_specs=[vmem] * len(shapes),
        scratch_shapes=scratch,
        compiler_params=pltpu.CompilerParams(vmem_limit_bytes=28 << 20),
        cost_estimate=pl.CostEstimate(flops=0, bytes_accessed=0, transcendentals=0),
        name=name,
    )(*operands)
    return out[0] if len(out) == 1 else out


def reduce_over_depth(parts):
    own, low, up, down, high = parts
    up, down = by_depth(up, 1), by_depth(down, -1)
    up, down = lax.optimization_barrier((up, down))
    up2 = by_depth(low + up[16:32], 1)
    down2 = by_depth(high + down[0:16], -1)
    up2, down2 = lax.optimization_barrier((up2, down2))
    return jnp.concatenate([own[0:16] + down[16:32] + up2, own[16:32] + up[0:16] + down2])


def on_device(left_tiles, right_tiles, square_tiles, pairs, counts):
    row, col = lax.axis_index("row"), lax.axis_index("col")
    core = col % 2
    place = jnp.stack([row % 2 - core, core, lax.axis_index("depth")]).astype(jnp.int32)
    pattern, limits = pairs[0, 0, 0], counts[0, 0, 0]

    right = right_tiles[0, 0, 0, 0].reshape(TILES, 32, 128)
    left = left_tiles[0, 0, 0].reshape(TILES, 32, 128)

    args = (place, pattern, limits)
    choices = [(i, i) for i in range(4)]
    other0 = swap_zh(right)
    same1, same3, same2 = by_y(right, -1), by_y(right, 1), by_y(right, 2)
    twin0 = swap_core(left)
    acc = add_sections([(0, False, 0, [(0, 0)])], *args, [left], [right], None, "sections_a")
    other0, acc, left = lax.optimization_barrier((other0, acc, left))
    left1 = by_zl(left, -1)
    same1, same3, same2, other0, acc = lax.optimization_barrier((same1, same3, same2, other0, acc))

    other1, other3, other2 = by_y(other0, -1), by_y(other0, 1), by_y(other0, 2)
    left2 = by_zl(left1, -1)
    twin1 = swap_core(left1)
    acc = add_sections([(1, False, 0, [(1, 0)])], *args, [left1], [same1], acc, "sections_b")
    other1, other3, left2, acc = lax.optimization_barrier((other1, other3, left2, acc))

    left3 = by_zl(left2, -1)
    twin2 = swap_core(left2)
    other = [other0, other1, other2, other3]
    jobs = [(2, False, 0, [(2, 4)])] + [(k, True, k + 1, choices) for k in range(3)]
    last = [(3, False, 1, [(3, 5)]), (3, True, 0, choices)]
    acc, prepared = add_sections(
        jobs, *args, [left2, twin0, twin1, twin2], other + [same2, same3], acc, "sections_c", last
    )

    left3, acc = lax.optimization_barrier((left3, acc))
    twin3 = swap_core(left3)
    share = [
        add_sections(last, *args, [twin3, left3], [], acc, f"sections_e{h}", [], h, prepared) for h in range(2)
    ]
    share = [reduce_over_depth(half) for half in share]
    share = jnp.concatenate(share, axis=1)
    purified = 3.0 * square_tiles[0, 0] - 2.0 * share.reshape(TILES, 4096)
    return purified[None, None]


def solution(mesh):
    in_specs = (
        P("row", "col", "depth", None, None),
        P("row", "col", "depth", None, None, None),
        P("row", "col", "depth", None),
        P("row", "col", "depth", None, None, None),
        P("row", "col", "depth", None),
    )
    out_specs = P("row", "col", "depth", None)
    return jax.shard_map(
        on_device, mesh=mesh, in_specs=in_specs, out_specs=out_specs, check_vma=False
    )
```

```python
import functools

import jax
import jax.numpy as jnp
from jax import lax
from jax.experimental import pallas as pl
from jax.experimental.pallas import tpu as pltpu
from jax.sharding import PartitionSpec as P

AXES = ("row", "col", "depth")
F32 = jnp.float32
BF16 = jnp.bfloat16
TILES = 32
SLOTS = 128
UNROLL = 32
PARTS = ((0, 32), (32, 48), (48, 80), (80, 112), (112, 128))


def moved(x, target):
    pairs = []
    for y in range(4):
        for zh in range(2):
            for zl in range(4):
                for c in range(2):
                    for d in range(4):
                        ty, th, tl, tc, td = target(y, zh, zl, c, d)
                        source = ((y * 2 + zh) * 8 + zl * 2 + c) * 4 + d
                        dest = ((ty % 4 * 2 + th % 2) * 8 + tl % 4 * 2 + tc % 2) * 4 + td % 4
                        pairs.append((source, dest))
    return lax.ppermute(x, AXES, pairs)


def by_y(x, k):
    return moved(x, lambda y, zh, zl, c, d: (y + k, zh, zl, c, d))


def by_zl(x, k):
    return moved(x, lambda y, zh, zl, c, d: (y, zh, zl + k, c, d))


def by_depth(x, k):
    return moved(x, lambda y, zh, zl, c, d: (y, zh, zl, c, d + k))


def swap_zh(x):
    return moved(x, lambda y, zh, zl, c, d: (y, zh + 1, zl, c, d))


def swap_core(x):
    return moved(x, lambda y, zh, zl, c, d: (y, zh, zl, c + 1, d))


def split(p):
    high = p.astype(BF16).astype(F32)
    return high, p - high


def section_kernel(jobs, later, n_left, n_right, n_made, has_acc, half, *refs):
    def take(n):
        nonlocal refs
        taken, refs = refs[:n], refs[n:]
        return taken

    place, pairs, counts = take(3)
    lefts, rights, made = take(n_left), take(n_right), take(n_made)
    start = take(1) if has_acc else ()
    outs = take(len(PARTS)) if half is not None else ()
    out = take(1)[0]
    splits = take(len(later))
    a3 = take(1)[0]
    if rights:
        rows, b3 = take(2)
    shift, core, depth = place[0], place[1], place[2]
    lane = lax.broadcasted_iota(jnp.int32, (32, 128), 1) < 64
    height = out.shape[1]
    lane_left = lane[:height]

    def section(job):
        k, odd = job[0], job[1]
        return lax.rem(2 * k + 9 - 2 * core, 8) if odd else 2 * k

    def split_left(left, t):
        p = left[t] if half is None else left[t, height * half : height * half + height]
        h, low = split(p)
        hr = pltpu.roll(h, 64, 1)
        lr = pltpu.roll(low, 64, 1)
        a3[t, 0:height, 0:128] = jnp.where(lane_left, h, hr).astype(BF16)
        a3[t, height : 2 * height, 0:128] = jnp.where(lane_left, hr, h).astype(BF16)
        a3[t, 0:height, 128:256] = jnp.where(lane_left, low, lr).astype(BF16)
        a3[t, height : 2 * height, 128:256] = jnp.where(lane_left, lr, low).astype(BF16)

    def split_right(job, target):
        k, _, _, choices = job

        def interleave(ref):
            @pl.loop(0, TILES, unroll=4)
            def _(t):
                r = ref[t]
                rr = pltpu.roll(r, 64, 1)
                rows[t, pl.ds(0, 32, stride=2)] = jnp.where(lane, r, rr)
                rows[t, pl.ds(1, 32, stride=2)] = jnp.where(lane, rr, r)

        if len(choices) == 1:
            interleave(rights[choices[0][1]])
        else:
            want = lax.rem(k + shift + 4, 4)
            for offset, index in choices:
                pl.when(want == offset)(functools.partial(interleave, rights[index]))

        @pl.loop(0, TILES, unroll=4)
        def _(t):
            h, low = split(rows[t])
            h = h.astype(BF16)
            low = low.astype(BF16)
            target[t, 0:64] = h
            target[t, 64:128] = low
            target[t, 128:192] = h
            target[t, 192:256] = low

    if not has_acc:
        out[...] = jnp.zeros_like(out)
    elif half is None:
        out[...] = start[0][...]
    else:
        out[...] = start[0][:, height * half : height * half + height]
    for j, job in enumerate(jobs):
        left = lefts[job[2]]

        @pl.loop(0, TILES, unroll=4)
        def _(t):
            split_left(left, t)

        if made:
            weights = made[j]
        else:
            weights = b3
            split_right(job, weights)
        s = section(job)
        live = counts[s]

        @pl.loop(0, (live + UNROLL - 1) // UNROLL)
        def _(block):
            sums, slots = [], []
            for u in range(UNROLL):
                p = block * UNROLL + u
                c = jnp.dot(a3[pairs[s, 0, p]], weights[pairs[s, 1, p]], preferred_element_type=F32)
                sums.append(jnp.where(lane_left, c[0:height], c[height : 2 * height]))
                g = lax.rem(pairs[s, 2, p] + (4 - depth) * 32, SLOTS)
                slots.append(jnp.where(p < live, g, SLOTS))
            for u in range(UNROLL):
                out[slots[u]] += sums[u]

    for job, target in zip(later, splits):
        split_right(job, target)
    for ref, (first, last) in zip(outs, PARTS):
        ref[...] = out[first:last]


def add_sections(jobs, place, pattern, limits, lefts, rights, acc, name, later=[], half=None, made=[]):
    smem = pl.BlockSpec(memory_space=pltpu.SMEM)
    vmem = pl.BlockSpec(memory_space=pltpu.VMEM)
    operands = [*lefts, *rights, *made] + ([] if acc is None else [acc])
    height = 32 if half is None else 16
    sums = (SLOTS + 1, height, 128)
    shapes = [jax.ShapeDtypeStruct(sums, F32)]
    shapes += [jax.ShapeDtypeStruct((TILES, 256, 128), BF16) for _ in later]
    scratch = [pltpu.VMEM((TILES, 2 * height, 256), BF16)]
    if rights:
        scratch += [pltpu.VMEM((TILES, 64, 128), F32), pltpu.VMEM((TILES, 256, 128), BF16)]
    if half is not None:
        shapes = [jax.ShapeDtypeStruct((last - first, height, 128), F32) for first, last in PARTS]
        scratch = [pltpu.VMEM(sums, F32)] + scratch
    out = pl.pallas_call(
        functools.partial(
            section_kernel, jobs, later, len(lefts), len(rights), len(made), acc is not None, half
        ),
        out_shape=shapes,
        in_specs=[smem] * 3 + [vmem] * len(operands),
        out_specs=[vmem] * len(shapes),
        scratch_shapes=scratch,
        compiler_params=pltpu.CompilerParams(vmem_limit_bytes=28 << 20),
        cost_estimate=pl.CostEstimate(flops=0, bytes_accessed=0, transcendentals=0),
        name=name,
    )(place, pattern, limits, *operands)
    return out[0] if len(out) == 1 else out


def reduce_over_depth(parts):
    own, low, up, down, high = parts
    up, down = by_depth(up, 1), by_depth(down, -1)
    up, down = lax.optimization_barrier((up, down))
    up2 = by_depth(low + up[16:32], 1)
    down2 = by_depth(high + down[0:16], -1)
    up2, down2 = lax.optimization_barrier((up2, down2))
    return jnp.concatenate([own[0:16] + down[16:32] + up2, own[16:32] + up[0:16] + down2])


def on_device(left_tiles, right_tiles, square_tiles, pairs, counts):
    row, col = lax.axis_index("row"), lax.axis_index("col")
    core = col % 2
    place = jnp.stack([row % 2 - core, core, lax.axis_index("depth")]).astype(jnp.int32)
    pattern, limits = pairs[0, 0, 0], counts[0, 0, 0]

    right = right_tiles[0, 0, 0, 0].reshape(TILES, 32, 128)
    left = left_tiles[0, 0, 0].reshape(TILES, 32, 128)

    args = (place, pattern, limits)
    choices = [(i, i) for i in range(4)]
    other0 = swap_zh(right)
    same1, same3, same2 = by_y(right, -1), by_y(right, 1), by_y(right, 2)
    twin0 = swap_core(left)
    acc = add_sections([(0, False, 0, [(0, 0)])], *args, [left], [right], None, "sections_a")
    other0, acc, left = lax.optimization_barrier((other0, acc, left))
    left1 = by_zl(left, -1)
    same1, same3, same2, other0, acc = lax.optimization_barrier((same1, same3, same2, other0, acc))

    other1, other3, other2 = by_y(other0, -1), by_y(other0, 1), by_y(other0, 2)
    left2 = by_zl(left1, -1)
    twin1 = swap_core(left1)
    even3, odd3 = (3, False, 1, [(3, 1)]), (3, True, 0, choices)
    acc, made_even = add_sections(
        [(1, False, 0, [(1, 0)])], *args, [left1], [same1, same3], acc, "sections_b", [even3]
    )
    other1, other3, left2, acc = lax.optimization_barrier((other1, other3, left2, acc))

    left3 = by_zl(left2, -1)
    twin2 = swap_core(left2)
    acc = add_sections([(2, False, 0, [(2, 0)])], *args, [left2], [same2], acc, "sections_c")
    other2, acc = lax.optimization_barrier((other2, acc))
    other = [other0, other1, other2, other3]
    jobs = [(k, True, k, choices) for k in range(3)]
    acc, made_odd = add_sections(jobs, *args, [twin0, twin1, twin2], other, acc, "sections_d", [odd3])

    left3, acc = lax.optimization_barrier((left3, acc))
    twin3 = swap_core(left3)
    made, lefts = [made_even, made_odd], [twin3, left3]
    share = [
        add_sections([even3, odd3], *args, lefts, [], acc, f"sections_e{h}", [], h, made) for h in range(2)
    ]
    share = [reduce_over_depth(half) for half in share]
    share = jnp.concatenate(share, axis=1)
    purified = 3.0 * square_tiles[0, 0] - 2.0 * share.reshape(TILES, 4096)
    return purified[None, None]


def solution(mesh):
    in_specs = (
        P("row", "col", "depth", None, None),
        P("row", "col", "depth", None, None, None),
        P("row", "col", "depth", None),
        P("row", "col", "depth", None, None, None),
        P("row", "col", "depth", None),
    )
    out_specs = P("row", "col", "depth", None)
    return jax.shard_map(
        on_device, mesh=mesh, in_specs=in_specs, out_specs=out_specs, check_vma=False
    )
```

```python
import functools

import jax
import jax.numpy as jnp
from jax import lax
from jax.experimental import pallas as pl
from jax.experimental.pallas import tpu as pltpu
from jax.sharding import PartitionSpec as P

AXES = ("row", "col", "depth")
F32 = jnp.float32
BF16 = jnp.bfloat16
TILES = 32
SLOTS = 128
UNROLL = 32
PARTS = ((0, 32), (32, 48), (48, 80), (80, 112), (112, 128))


def moved(x, target):
    pairs = []
    for y in range(4):
        for zh in range(2):
            for zl in range(4):
                for c in range(2):
                    for d in range(4):
                        ty, th, tl, tc, td = target(y, zh, zl, c, d)
                        source = ((y * 2 + zh) * 8 + zl * 2 + c) * 4 + d
                        dest = ((ty % 4 * 2 + th % 2) * 8 + tl % 4 * 2 + tc % 2) * 4 + td % 4
                        pairs.append((source, dest))
    return lax.ppermute(x, AXES, pairs)


def by_y(x, k):
    return moved(x, lambda y, zh, zl, c, d: (y + k, zh, zl, c, d))


def by_zl(x, k):
    return moved(x, lambda y, zh, zl, c, d: (y, zh, zl + k, c, d))


def by_depth(x, k):
    return moved(x, lambda y, zh, zl, c, d: (y, zh, zl, c, d + k))


def swap_zh(x):
    return moved(x, lambda y, zh, zl, c, d: (y, zh + 1, zl, c, d))


def swap_core(x):
    return moved(x, lambda y, zh, zl, c, d: (y, zh, zl, c + 1, d))


def split(p):
    high = p.astype(BF16).astype(F32)
    return high, p - high


def section_kernel(jobs, later, n_left, n_right, n_made, has_acc, half, *refs):
    def take(n):
        nonlocal refs
        taken, refs = refs[:n], refs[n:]
        return taken

    place, pairs, counts = take(3)
    lefts, rights, made = take(n_left), take(n_right), take(n_made)
    start = take(1) if has_acc else ()
    outs = take(len(PARTS)) if half is not None else ()
    out = take(1)[0]
    splits = take(len(later))
    a3, b3 = take(2)
    rows = take(1)[0] if rights else None
    shift, core, depth = place[0], place[1], place[2]
    lane = lax.broadcasted_iota(jnp.int32, (32, 128), 1) < 64
    height = out.shape[1]
    lane_left = lane[:height]

    def section(job):
        k, odd = job[0], job[1]
        return lax.rem(2 * k + 9 - 2 * core, 8) if odd else 2 * k

    def split_left(left, t):
        p = left[t] if half is None else left[t, height * half : height * half + height]
        h, low = split(p)
        hr = pltpu.roll(h, 64, 1)
        lr = pltpu.roll(low, 64, 1)
        a3[t, 0:height] = jnp.where(lane_left, h, hr).astype(BF16)
        a3[t, height : 2 * height] = jnp.where(lane_left, hr, h).astype(BF16)
        a3[t, 2 * height : 3 * height] = jnp.where(lane_left, low, lr).astype(BF16)
        a3[t, 3 * height : 4 * height] = jnp.where(lane_left, lr, low).astype(BF16)

    def split_right(job, target):
        k, _, _, choices = job

        def interleave(ref):
            @pl.loop(0, TILES, unroll=4)
            def _(t):
                r = ref[t]
                rr = pltpu.roll(r, 64, 1)
                rows[t, pl.ds(0, 32, stride=2)] = jnp.where(lane, r, rr)
                rows[t, pl.ds(1, 32, stride=2)] = jnp.where(lane, rr, r)

        if len(choices) == 1:
            interleave(rights[choices[0][1]])
        else:
            want = lax.rem(k + shift + 4, 4)
            for offset, index in choices:
                pl.when(want == offset)(functools.partial(interleave, rights[index]))

        @pl.loop(0, TILES, unroll=4)
        def _(t):
            h, low = split(rows[t])
            target[t, 0:64] = h.astype(BF16)
            target[t, 64:128] = low.astype(BF16)

    if not has_acc:
        out[...] = jnp.zeros_like(out)
    elif half is None:
        out[...] = start[0][...]
    else:
        out[...] = start[0][:, height * half : height * half + height]
    def split_panels(j):
        left = lefts[jobs[j][2]]

        @pl.loop(0, TILES, unroll=4)
        def _(t):
            split_left(left, t)
            if made:
                b3[t] = made[j][t]

        if not made:
            split_right(jobs[j], b3)

    def add_products(s):
        live = counts[s]

        @pl.loop(0, (live + UNROLL - 1) // UNROLL)
        def _(block):
            sums, slots = [], []
            for u in range(UNROLL):
                p = block * UNROLL + u
                c = jnp.dot(a3[pairs[s, 0, p]], b3[pairs[s, 1, p]], preferred_element_type=F32)
                c = c[0 : 2 * height] + c[2 * height : 4 * height]
                sums.append(jnp.where(lane_left, c[0:height], c[height : 2 * height]))
                g = lax.rem(pairs[s, 2, p] + (4 - depth) * 32, SLOTS)
                slots.append(jnp.where(p < live, g, SLOTS))
            for u in range(UNROLL):
                out[slots[u]] += sums[u]

    if len(jobs) == 1:
        split_panels(0)
        add_products(section(jobs[0]))
    else:

        @pl.loop(0, len(jobs))
        def _(now):
            s = jnp.int32(0)
            for j, job in enumerate(jobs):
                s = jnp.where(now == j, section(job), s)
                pl.when(now == j)(functools.partial(split_panels, j))
            add_products(s)

    for job, target in zip(later, splits):
        split_right(job, target)
    for ref, (first, last) in zip(outs, PARTS):
        ref[...] = out[first:last]


def add_sections(jobs, place, pattern, limits, lefts, rights, acc, name, later=[], half=None, made=[]):
    smem = pl.BlockSpec(memory_space=pltpu.SMEM)
    vmem = pl.BlockSpec(memory_space=pltpu.VMEM)
    operands = [*lefts, *rights, *made] + ([] if acc is None else [acc])
    height = 32 if half is None else 16
    sums = (SLOTS + 1, height, 128)
    shapes = [jax.ShapeDtypeStruct(sums, F32)]
    shapes += [jax.ShapeDtypeStruct((TILES, 128, 128), BF16) for _ in later]
    scratch = [pltpu.VMEM((TILES, 4 * height, 128), BF16), pltpu.VMEM((TILES, 128, 128), BF16)]
    if rights:
        scratch.append(pltpu.VMEM((TILES, 64, 128), F32))
    if half is not None:
        shapes = [jax.ShapeDtypeStruct((last - first, height, 128), F32) for first, last in PARTS]
        scratch = [pltpu.VMEM(sums, F32)] + scratch
    out = pl.pallas_call(
        functools.partial(
            section_kernel, jobs, later, len(lefts), len(rights), len(made), acc is not None, half
        ),
        out_shape=shapes,
        in_specs=[smem] * 3 + [vmem] * len(operands),
        out_specs=[vmem] * len(shapes),
        scratch_shapes=scratch,
        compiler_params=pltpu.CompilerParams(vmem_limit_bytes=28 << 20),
        cost_estimate=pl.CostEstimate(flops=0, bytes_accessed=0, transcendentals=0),
        name=name,
    )(place, pattern, limits, *operands)
    return out[0] if len(out) == 1 else out


def reduce_over_depth(parts):
    own, low, up, down, high = parts
    up, down = by_depth(up, 1), by_depth(down, -1)
    up, down = lax.optimization_barrier((up, down))
    up2 = by_depth(low + up[16:32], 1)
    down2 = by_depth(high + down[0:16], -1)
    up2, down2 = lax.optimization_barrier((up2, down2))
    return jnp.concatenate([own[0:16] + down[16:32] + up2, own[16:32] + up[0:16] + down2])


def on_device(left_tiles, right_tiles, square_tiles, pairs, counts):
    row, col = lax.axis_index("row"), lax.axis_index("col")
    core = col % 2
    place = jnp.stack([row % 2 - core, core, lax.axis_index("depth")]).astype(jnp.int32)
    pattern, limits = pairs[0, 0, 0], counts[0, 0, 0]

    right = right_tiles[0, 0, 0, 0].reshape(TILES, 32, 128)
    left = left_tiles[0, 0, 0].reshape(TILES, 32, 128)

    args = (place, pattern, limits)
    choices = [(i, i) for i in range(4)]
    other0 = swap_zh(right)
    same1, same3, same2 = by_y(right, -1), by_y(right, 1), by_y(right, 2)
    twin0 = swap_core(left)
    acc = add_sections([(0, False, 0, [(0, 0)])], *args, [left], [right], None, "sections_a")
    other0, acc, left = lax.optimization_barrier((other0, acc, left))
    left1 = by_zl(left, -1)
    same1, same3, same2, other0, acc = lax.optimization_barrier((same1, same3, same2, other0, acc))

    other1, other3, other2 = by_y(other0, -1), by_y(other0, 1), by_y(other0, 2)
    left2 = by_zl(left1, -1)
    twin1 = swap_core(left1)
    even3, odd3 = (3, False, 1, [(3, 1)]), (3, True, 0, choices)
    acc, made_even = add_sections(
        [(1, False, 0, [(1, 0)])], *args, [left1], [same1, same3], acc, "sections_b", [even3]
    )
    other1, other3, left2, acc = lax.optimization_barrier((other1, other3, left2, acc))

    left3 = by_zl(left2, -1)
    twin2 = swap_core(left2)
    acc = add_sections([(2, False, 0, [(2, 0)])], *args, [left2], [same2], acc, "sections_c")
    other2, acc = lax.optimization_barrier((other2, acc))
    other = [other0, other1, other2, other3]
    jobs = [(k, True, k, choices) for k in range(3)]
    acc, made_odd = add_sections(jobs, *args, [twin0, twin1, twin2], other, acc, "sections_d", [odd3])

    left3, acc = lax.optimization_barrier((left3, acc))
    twin3 = swap_core(left3)
    made, lefts = [made_even, made_odd], [twin3, left3]
    share = [
        add_sections([even3, odd3], *args, lefts, [], acc, f"sections_e{h}", [], h, made) for h in range(2)
    ]
    share = [reduce_over_depth(half) for half in share]
    share = jnp.concatenate(share, axis=1)
    purified = 3.0 * square_tiles[0, 0] - 2.0 * share.reshape(TILES, 4096)
    return purified[None, None]


def solution(mesh):
    in_specs = (
        P("row", "col", "depth", None, None),
        P("row", "col", "depth", None, None, None),
        P("row", "col", "depth", None),
        P("row", "col", "depth", None, None, None),
        P("row", "col", "depth", None),
    )
    out_specs = P("row", "col", "depth", None)
    return jax.shard_map(
        on_device, mesh=mesh, in_specs=in_specs, out_specs=out_specs, check_vma=False
    )
```

```python
import functools

import jax
import jax.numpy as jnp
from jax import lax
from jax.experimental import pallas as pl
from jax.experimental.pallas import tpu as pltpu
from jax.sharding import PartitionSpec as P

AXES = ("row", "col", "depth")
F32 = jnp.float32
BF16 = jnp.bfloat16
TILES = 32
SLOTS = 128
UNROLL = 32
PARTS = ((0, 32), (32, 48), (48, 80), (80, 112), (112, 128))


def moved(x, target):
    pairs = []
    for y in range(4):
        for zh in range(2):
            for zl in range(4):
                for c in range(2):
                    for d in range(4):
                        ty, th, tl, tc, td = target(y, zh, zl, c, d)
                        source = ((y * 2 + zh) * 8 + zl * 2 + c) * 4 + d
                        dest = ((ty % 4 * 2 + th % 2) * 8 + tl % 4 * 2 + tc % 2) * 4 + td % 4
                        pairs.append((source, dest))
    return lax.ppermute(x, AXES, pairs)


def by_y(x, k):
    return moved(x, lambda y, zh, zl, c, d: (y + k, zh, zl, c, d))


def by_zl(x, k):
    return moved(x, lambda y, zh, zl, c, d: (y, zh, zl + k, c, d))


def by_depth(x, k):
    return moved(x, lambda y, zh, zl, c, d: (y, zh, zl, c, d + k))


def swap_zh(x):
    return moved(x, lambda y, zh, zl, c, d: (y, zh + 1, zl, c, d))


def swap_core(x):
    return moved(x, lambda y, zh, zl, c, d: (y, zh, zl, c + 1, d))


def split(p):
    high = p.astype(BF16).astype(F32)
    return high, p - high


def section_kernel(jobs, later, n_left, n_right, n_made, has_acc, half, *refs):
    def take(n):
        nonlocal refs
        taken, refs = refs[:n], refs[n:]
        return taken

    place, pairs, counts = take(3)
    lefts, rights, made = take(n_left), take(n_right), take(n_made)
    start = take(1) if has_acc else ()
    outs = take(len(PARTS)) if half is not None else ()
    out = take(1)[0]
    splits = take(len(later))
    a3, b3 = take(2)
    rows = take(1)[0] if rights else None
    shift, core, depth = place[0], place[1], place[2]
    lane = lax.broadcasted_iota(jnp.int32, (32, 128), 1) < 64
    height = out.shape[1]
    lane_left = lane[:height]

    def section(job):
        k, odd = job[0], job[1]
        return lax.rem(2 * k + 9 - 2 * core, 8) if odd else 2 * k

    def split_left(left, t):
        p = left[t] if half is None else left[t, height * half : height * half + height]
        h, low = split(p)
        hr = pltpu.roll(h, 64, 1)
        lr = pltpu.roll(low, 64, 1)
        a3[t, 0:height] = jnp.where(lane_left, h, hr).astype(BF16)
        a3[t, height : 2 * height] = jnp.where(lane_left, hr, h).astype(BF16)
        a3[t, 2 * height : 3 * height] = jnp.where(lane_left, low, lr).astype(BF16)
        a3[t, 3 * height : 4 * height] = jnp.where(lane_left, lr, low).astype(BF16)

    def split_right(job, target):
        k, _, _, choices = job

        def interleave(ref):
            @pl.loop(0, TILES, unroll=4)
            def _(t):
                r = ref[t]
                rr = pltpu.roll(r, 64, 1)
                rows[t, pl.ds(0, 32, stride=2)] = jnp.where(lane, r, rr)
                rows[t, pl.ds(1, 32, stride=2)] = jnp.where(lane, rr, r)

        if len(choices) == 1:
            interleave(rights[choices[0][1]])
        else:
            want = lax.rem(k + shift + 4, 4)
            for offset, index in choices:
                pl.when(want == offset)(functools.partial(interleave, rights[index]))

        @pl.loop(0, TILES, unroll=4)
        def _(t):
            h, low = split(rows[t])
            target[t, 0:64] = h.astype(BF16)
            target[t, 64:128] = low.astype(BF16)

    if not has_acc:
        out[...] = jnp.zeros_like(out)
    elif half is None:
        out[...] = start[0][...]
    else:
        out[...] = start[0][:, height * half : height * half + height]
    def split_panels(j):
        left = lefts[jobs[j][2]]

        @pl.loop(0, TILES, unroll=4)
        def _(t):
            split_left(left, t)
            if made:
                b3[t] = made[j][t]

        if not made:
            split_right(jobs[j], b3)

    def add_products(s):
        live = counts[s]

        @pl.loop(0, (live + UNROLL - 1) // UNROLL)
        def _(block):
            sums, slots = [], []
            for u in range(UNROLL):
                p = block * UNROLL + u
                c = jnp.dot(a3[pairs[s, 0, p]], b3[pairs[s, 1, p]], preferred_element_type=F32)
                c = c[0 : 2 * height] + c[2 * height : 4 * height]
                sums.append(jnp.where(lane_left, c[0:height], c[height : 2 * height]))
                g = lax.rem(pairs[s, 2, p] + (4 - depth) * 32, SLOTS)
                slots.append(jnp.where(p < live, g, SLOTS))
            for u in range(UNROLL):
                out[slots[u]] += sums[u]

    if len(jobs) == 1:
        split_panels(0)
        add_products(section(jobs[0]))
    else:

        @pl.loop(0, len(jobs))
        def _(now):
            s = jnp.int32(0)
            for j, job in enumerate(jobs):
                s = jnp.where(now == j, section(job), s)
                pl.when(now == j)(functools.partial(split_panels, j))
            add_products(s)

    for job, target in zip(later, splits):
        split_right(job, target)
    for ref, (first, last) in zip(outs, PARTS):
        ref[...] = out[first:last]


def add_sections(jobs, place, pattern, limits, lefts, rights, acc, name, later=[], half=None, made=[]):
    smem = pl.BlockSpec(memory_space=pltpu.SMEM)
    vmem = pl.BlockSpec(memory_space=pltpu.VMEM)
    operands = [*lefts, *rights, *made] + ([] if acc is None else [acc])
    height = 32 if half is None else 16
    sums = (SLOTS + 1, height, 128)
    shapes = [jax.ShapeDtypeStruct(sums, F32)]
    shapes += [jax.ShapeDtypeStruct((TILES, 128, 128), BF16) for _ in later]
    scratch = [pltpu.VMEM((TILES, 4 * height, 128), BF16), pltpu.VMEM((TILES, 128, 128), BF16)]
    if rights:
        scratch.append(pltpu.VMEM((TILES, 64, 128), F32))
    if half is not None:
        shapes = [jax.ShapeDtypeStruct((last - first, height, 128), F32) for first, last in PARTS]
        scratch = [pltpu.VMEM(sums, F32)] + scratch
    out = pl.pallas_call(
        functools.partial(
            section_kernel, jobs, later, len(lefts), len(rights), len(made), acc is not None, half
        ),
        out_shape=shapes,
        in_specs=[smem] * 3 + [vmem] * len(operands),
        out_specs=[vmem] * len(shapes),
        scratch_shapes=scratch,
        compiler_params=pltpu.CompilerParams(vmem_limit_bytes=28 << 20),
        cost_estimate=pl.CostEstimate(flops=0, bytes_accessed=0, transcendentals=0),
        name=name,
    )(place, pattern, limits, *operands)
    return out[0] if len(out) == 1 else out


def reduce_over_depth(parts):
    own, low, up, down, high = parts
    up, down = by_depth(up, 1), by_depth(down, -1)
    up, down = lax.optimization_barrier((up, down))
    up2 = by_depth(low + up[16:32], 1)
    down2 = by_depth(high + down[0:16], -1)
    up2, down2 = lax.optimization_barrier((up2, down2))
    return jnp.concatenate([own[0:16] + down[16:32] + up2, own[16:32] + up[0:16] + down2])


def on_device(left_tiles, right_tiles, square_tiles, pairs, counts):
    row, col = lax.axis_index("row"), lax.axis_index("col")
    core = col % 2
    place = jnp.stack([row % 2 - core, core, lax.axis_index("depth")]).astype(jnp.int32)
    pattern, limits = pairs[0, 0, 0], counts[0, 0, 0]

    right = right_tiles[0, 0, 0, 0].reshape(TILES, 32, 128)
    left = left_tiles[0, 0, 0].reshape(TILES, 32, 128)

    args = (place, pattern, limits)
    choices = [(i, i) for i in range(4)]
    other0 = swap_zh(right)
    same1, same3, same2 = by_y(right, -1), by_y(right, 1), by_y(right, 2)
    twin0 = swap_core(left)
    acc = add_sections([(0, False, 0, [(0, 0)])], *args, [left], [right], None, "sections_a")
    other0, acc, left = lax.optimization_barrier((other0, acc, left))
    left1 = by_zl(left, -1)
    same1, same3, same2, other0, acc = lax.optimization_barrier((same1, same3, same2, other0, acc))

    other1, other3, other2 = by_y(other0, -1), by_y(other0, 1), by_y(other0, 2)
    left2 = by_zl(left1, -1)
    twin1 = swap_core(left1)
    even3, odd3 = (3, False, 0, [(3, 1)]), (3, True, 0, choices)
    acc, made_even = add_sections(
        [(1, False, 0, [(1, 0)])], *args, [left1], [same1, same3], acc, "sections_b", [even3]
    )
    near = [(0, 0), (1, 1), (3, 2)]
    acc = add_sections([(0, True, 0, near)], *args, [twin0], [other0, other1, other3], acc, "sections_c")
    other1, other3, left2, acc = lax.optimization_barrier((other1, other3, left2, acc))

    left3 = by_zl(left2, -1)
    acc = add_sections([(2, False, 0, [(2, 0)])], *args, [left2], [same2], acc, "sections_d")
    twin2 = swap_core(left2)
    other = [other0, other1, other2, other3]
    jobs = [(k, True, k - 1, choices) for k in (1, 2)]
    acc, made_odd = add_sections(jobs, *args, [twin1, twin2], other, acc, "sections_e", [odd3])

    left3, acc = lax.optimization_barrier((left3, acc))
    twin3 = swap_core(left3)
    acc = add_sections([even3], *args, [left3], [], acc, "sections_f", made=[made_even])
    share = [
        add_sections([odd3], *args, [twin3], [], acc, f"sections_g{h}", [], h, [made_odd]) for h in range(2)
    ]
    share = [reduce_over_depth(half) for half in share]
    share = jnp.concatenate(share, axis=1)
    purified = 3.0 * square_tiles[0, 0] - 2.0 * share.reshape(TILES, 4096)
    return purified[None, None]


def solution(mesh):
    in_specs = (
        P("row", "col", "depth", None, None),
        P("row", "col", "depth", None, None, None),
        P("row", "col", "depth", None),
        P("row", "col", "depth", None, None, None),
        P("row", "col", "depth", None),
    )
    out_specs = P("row", "col", "depth", None)
    return jax.shard_map(
        on_device, mesh=mesh, in_specs=in_specs, out_specs=out_specs, check_vma=False
    )
```

```python
import functools

import jax
import jax.numpy as jnp
from jax import lax
from jax.experimental import pallas as pl
from jax.experimental.pallas import tpu as pltpu
from jax.sharding import PartitionSpec as P

AXES = ("row", "col", "depth")
F32 = jnp.float32
BF16 = jnp.bfloat16
TILES = 32
SLOTS = 128
UNROLL = 32
PARTS = ((0, 32), (32, 48), (48, 80), (80, 112), (112, 128))


def moved(x, target):
    pairs = []
    for y in range(4):
        for zh in range(2):
            for zl in range(4):
                for c in range(2):
                    for d in range(4):
                        ty, th, tl, tc, td = target(y, zh, zl, c, d)
                        source = ((y * 2 + zh) * 8 + zl * 2 + c) * 4 + d
                        dest = ((ty % 4 * 2 + th % 2) * 8 + tl % 4 * 2 + tc % 2) * 4 + td % 4
                        pairs.append((source, dest))
    return lax.ppermute(x, AXES, pairs)


def by_y(x, k):
    return moved(x, lambda y, zh, zl, c, d: (y + k, zh, zl, c, d))


def by_zl(x, k):
    return moved(x, lambda y, zh, zl, c, d: (y, zh, zl + k, c, d))


def by_depth(x, k):
    return moved(x, lambda y, zh, zl, c, d: (y, zh, zl, c, d + k))


def swap_zh(x):
    return moved(x, lambda y, zh, zl, c, d: (y, zh + 1, zl, c, d))


def swap_core(x):
    return moved(x, lambda y, zh, zl, c, d: (y, zh, zl, c + 1, d))


def split(p):
    high = p.astype(BF16).astype(F32)
    return high, p - high


def section_kernel(jobs, later, n_left, n_right, n_made, has_acc, half, *refs):
    def take(n):
        nonlocal refs
        taken, refs = refs[:n], refs[n:]
        return taken

    place, pairs, counts = take(3)
    lefts, rights, made = take(n_left), take(n_right), take(n_made)
    start = take(1) if has_acc else ()
    outs = take(len(PARTS)) if half is not None else ()
    out = take(1)[0]
    splits = take(len(later))
    a3, b3 = take(2)
    rows = take(1)[0] if rights else None
    shift, core, depth = place[0], place[1], place[2]
    lane = lax.broadcasted_iota(jnp.int32, (32, 128), 1) < 64
    height = out.shape[1]
    lane_left = lane[:height]

    def section(job):
        k, odd = job[0], job[1]
        return lax.rem(2 * k + 9 - 2 * core, 8) if odd else 2 * k

    def split_left(left, t):
        p = left[t] if half is None else left[t, height * half : height * half + height]
        h, low = split(p)
        hr = pltpu.roll(h, 64, 1)
        lr = pltpu.roll(low, 64, 1)
        a3[t, 0:height] = jnp.where(lane_left, h, hr).astype(BF16)
        a3[t, height : 2 * height] = jnp.where(lane_left, hr, h).astype(BF16)
        a3[t, 2 * height : 3 * height] = jnp.where(lane_left, low, lr).astype(BF16)
        a3[t, 3 * height : 4 * height] = jnp.where(lane_left, lr, low).astype(BF16)

    def split_right(job, target):
        k, _, _, choices = job

        def interleave(ref):
            @pl.loop(0, TILES, unroll=4)
            def _(t):
                r = ref[t]
                rr = pltpu.roll(r, 64, 1)
                rows[t, pl.ds(0, 32, stride=2)] = jnp.where(lane, r, rr)
                rows[t, pl.ds(1, 32, stride=2)] = jnp.where(lane, rr, r)

        if len(choices) == 1:
            interleave(rights[choices[0][1]])
        else:
            want = lax.rem(k + shift + 4, 4)
            for offset, index in choices:
                pl.when(want == offset)(functools.partial(interleave, rights[index]))

        @pl.loop(0, TILES, unroll=4)
        def _(t):
            h, low = split(rows[t])
            target[t, 0:64] = h.astype(BF16)
            target[t, 64:128] = low.astype(BF16)

    if not has_acc:
        out[...] = jnp.zeros_like(out)
    elif half is None:
        out[...] = start[0][...]
    else:
        out[...] = start[0][:, height * half : height * half + height]
    def split_panels(j):
        left = lefts[jobs[j][2]]

        @pl.loop(0, TILES, unroll=4)
        def _(t):
            split_left(left, t)
            if made:
                b3[t] = made[j][t]

        if not made:
            split_right(jobs[j], b3)

    def add_products(s):
        live = counts[s]

        @pl.loop(0, (live + UNROLL - 1) // UNROLL)
        def _(block):
            sums, slots = [], []
            for u in range(UNROLL):
                p = block * UNROLL + u
                c = jnp.dot(a3[pairs[s, 0, p]], b3[pairs[s, 1, p]], preferred_element_type=F32)
                c = c[0 : 2 * height] + c[2 * height : 4 * height]
                sums.append(jnp.where(lane_left, c[0:height], c[height : 2 * height]))
                g = lax.rem(pairs[s, 2, p] + (4 - depth) * 32, SLOTS)
                slots.append(jnp.where(p < live, g, SLOTS))
            for u in range(UNROLL):
                out[slots[u]] += sums[u]

    if len(jobs) == 1:
        split_panels(0)
        add_products(section(jobs[0]))
    else:

        @pl.loop(0, len(jobs))
        def _(now):
            s = jnp.int32(0)
            for j, job in enumerate(jobs):
                s = jnp.where(now == j, section(job), s)
                pl.when(now == j)(functools.partial(split_panels, j))
            add_products(s)

    for job, target in zip(later, splits):
        split_right(job, target)
    for ref, (first, last) in zip(outs, PARTS):
        ref[...] = out[first:last]


def add_sections(jobs, place, pattern, limits, lefts, rights, acc, name, later=[], half=None, made=[]):
    smem = pl.BlockSpec(memory_space=pltpu.SMEM)
    vmem = pl.BlockSpec(memory_space=pltpu.VMEM)
    operands = [*lefts, *rights, *made] + ([] if acc is None else [acc])
    height = 32 if half is None else 16
    sums = (SLOTS + 1, height, 128)
    shapes = [jax.ShapeDtypeStruct(sums, F32)]
    shapes += [jax.ShapeDtypeStruct((TILES, 128, 128), BF16) for _ in later]
    scratch = [pltpu.VMEM((TILES, 4 * height, 128), BF16), pltpu.VMEM((TILES, 128, 128), BF16)]
    if rights:
        scratch.append(pltpu.VMEM((TILES, 64, 128), F32))
    if half is not None:
        shapes = [jax.ShapeDtypeStruct((last - first, height, 128), F32) for first, last in PARTS]
        scratch = [pltpu.VMEM(sums, F32)] + scratch
    out = pl.pallas_call(
        functools.partial(
            section_kernel, jobs, later, len(lefts), len(rights), len(made), acc is not None, half
        ),
        out_shape=shapes,
        in_specs=[smem] * 3 + [vmem] * len(operands),
        out_specs=[vmem] * len(shapes),
        scratch_shapes=scratch,
        compiler_params=pltpu.CompilerParams(vmem_limit_bytes=28 << 20),
        cost_estimate=pl.CostEstimate(flops=0, bytes_accessed=0, transcendentals=0),
        name=name,
    )(place, pattern, limits, *operands)
    return out[0] if len(out) == 1 else out


def reduce_over_depth(parts):
    own, low, up, down, high = parts
    up, down = by_depth(up, 1), by_depth(down, -1)
    up, down = lax.optimization_barrier((up, down))
    up2 = by_depth(low + up[16:32], 1)
    down2 = by_depth(high + down[0:16], -1)
    up2, down2 = lax.optimization_barrier((up2, down2))
    return jnp.concatenate([own[0:16] + down[16:32] + up2, own[16:32] + up[0:16] + down2])


def on_device(left_tiles, right_tiles, square_tiles, pairs, counts):
    row, col = lax.axis_index("row"), lax.axis_index("col")
    core = col % 2
    place = jnp.stack([row % 2 - core, core, lax.axis_index("depth")]).astype(jnp.int32)
    pattern, limits = pairs[0, 0, 0], counts[0, 0, 0]

    right = right_tiles[0, 0, 0, 0].reshape(TILES, 32, 128)
    left = left_tiles[0, 0, 0].reshape(TILES, 32, 128)

    args = (place, pattern, limits)
    choices = [(i, i) for i in range(4)]
    other0 = swap_zh(right)
    same1, same3, same2 = by_y(right, -1), by_y(right, 1), by_y(right, 2)
    twin0 = swap_core(left)
    acc = add_sections([(0, False, 0, [(0, 0)])], *args, [left], [right], None, "sections_a")
    other0, acc, left = lax.optimization_barrier((other0, acc, left))
    left1 = by_zl(left, -1)
    same1, same3, same2, other0, acc = lax.optimization_barrier((same1, same3, same2, other0, acc))

    other1, other3, other2 = by_y(other0, -1), by_y(other0, 1), by_y(other0, 2)
    left2 = by_zl(left1, -1)
    twin1 = swap_core(left1)
    even3, odd3 = (3, False, 0, [(3, 1)]), (3, True, 0, choices)
    acc, made_even = add_sections(
        [(1, False, 0, [(1, 0)])], *args, [left1], [same1, same3], acc, "sections_b", [even3]
    )
    other1, other3, left2, acc = lax.optimization_barrier((other1, other3, left2, acc))

    left3 = by_zl(left2, -1)
    jobs = [(2, False, 1, [(2, 3)]), (0, True, 0, [(0, 0), (1, 1), (3, 2)])]
    acc = add_sections(jobs, *args, [twin0, left2], [other0, other1, other3, same2], acc, "sections_c")
    twin2 = swap_core(left2)
    other = [other0, other1, other2, other3]
    jobs = [(k, True, k - 1, choices) for k in (1, 2)]
    acc, made_odd = add_sections(jobs, *args, [twin1, twin2], other, acc, "sections_d", [odd3])

    left3, acc = lax.optimization_barrier((left3, acc))
    twin3 = swap_core(left3)
    acc = add_sections([even3], *args, [left3], [], acc, "sections_e", made=[made_even])
    share = [
        add_sections([odd3], *args, [twin3], [], acc, f"sections_f{h}", [], h, [made_odd]) for h in range(2)
    ]
    share = [reduce_over_depth(half) for half in share]
    share = jnp.concatenate(share, axis=1)
    purified = 3.0 * square_tiles[0, 0] - 2.0 * share.reshape(TILES, 4096)
    return purified[None, None]


def solution(mesh):
    in_specs = (
        P("row", "col", "depth", None, None),
        P("row", "col", "depth", None, None, None),
        P("row", "col", "depth", None),
        P("row", "col", "depth", None, None, None),
        P("row", "col", "depth", None),
    )
    out_specs = P("row", "col", "depth", None)
    return jax.shard_map(
        on_device, mesh=mesh, in_specs=in_specs, out_specs=out_specs, check_vma=False
    )
```

```python
import functools

import jax
import jax.numpy as jnp
from jax import lax
from jax.experimental import pallas as pl
from jax.experimental.pallas import tpu as pltpu
from jax.sharding import PartitionSpec as P

AXES = ("row", "col", "depth")
F32 = jnp.float32
BF16 = jnp.bfloat16
TILES = 32
SLOTS = 128
UNROLL = 32
PARTS = ((0, 32), (32, 48), (48, 80), (80, 112), (112, 128))


def moved(x, target):
    pairs = []
    for y in range(4):
        for zh in range(2):
            for zl in range(4):
                for c in range(2):
                    for d in range(4):
                        ty, th, tl, tc, td = target(y, zh, zl, c, d)
                        source = ((y * 2 + zh) * 8 + zl * 2 + c) * 4 + d
                        dest = ((ty % 4 * 2 + th % 2) * 8 + tl % 4 * 2 + tc % 2) * 4 + td % 4
                        pairs.append((source, dest))
    return lax.ppermute(x, AXES, pairs)


def by_y(x, k):
    return moved(x, lambda y, zh, zl, c, d: (y + k, zh, zl, c, d))


def by_zl(x, k):
    return moved(x, lambda y, zh, zl, c, d: (y, zh, zl + k, c, d))


def by_depth(x, k):
    return moved(x, lambda y, zh, zl, c, d: (y, zh, zl, c, d + k))


def swap_zh(x):
    return moved(x, lambda y, zh, zl, c, d: (y, zh + 1, zl, c, d))


def swap_core(x):
    return moved(x, lambda y, zh, zl, c, d: (y, zh, zl, c + 1, d))


def split(p):
    high = p.astype(BF16).astype(F32)
    return high, p - high


def section_kernel(jobs, later, n_left, n_right, n_made, has_acc, half, *refs):
    def take(n):
        nonlocal refs
        taken, refs = refs[:n], refs[n:]
        return taken

    place, pairs, counts = take(3)
    lefts, rights, made = take(n_left), take(n_right), take(n_made)
    start = take(1) if has_acc else ()
    outs = take(len(PARTS)) if half is not None else ()
    out = take(1)[0]
    splits = take(len(later))
    a3, b3 = take(2)
    rows = take(1)[0] if rights else None
    shift, core, depth = place[0], place[1], place[2]
    lane = lax.broadcasted_iota(jnp.int32, (32, 128), 1) < 64
    height = out.shape[1]
    lane_left = lane[:height]

    def section(job):
        k, odd = job[0], job[1]
        return lax.rem(2 * k + 9 - 2 * core, 8) if odd else 2 * k

    def split_left(left, t):
        p = left[t] if half is None else left[t, height * half : height * half + height]
        h, low = split(p)
        hr = pltpu.roll(h, 64, 1)
        lr = pltpu.roll(low, 64, 1)
        a3[t, 0:height] = jnp.where(lane_left, h, hr).astype(BF16)
        a3[t, height : 2 * height] = jnp.where(lane_left, hr, h).astype(BF16)
        a3[t, 2 * height : 3 * height] = jnp.where(lane_left, low, lr).astype(BF16)
        a3[t, 3 * height : 4 * height] = jnp.where(lane_left, lr, low).astype(BF16)

    def split_right(job, target):
        k, _, _, choices = job

        def interleave(ref):
            @pl.loop(0, TILES, unroll=4)
            def _(t):
                r = ref[t]
                rr = pltpu.roll(r, 64, 1)
                rows[t, pl.ds(0, 32, stride=2)] = jnp.where(lane, r, rr)
                rows[t, pl.ds(1, 32, stride=2)] = jnp.where(lane, rr, r)

        if len(choices) == 1:
            interleave(rights[choices[0][1]])
        else:
            want = lax.rem(k + shift + 4, 4)
            for offset, index in choices:
                pl.when(want == offset)(functools.partial(interleave, rights[index]))

        @pl.loop(0, TILES, unroll=4)
        def _(t):
            h, low = split(rows[t])
            target[t, 0:64] = h.astype(BF16)
            target[t, 64:128] = low.astype(BF16)

    if not has_acc:
        out[...] = jnp.zeros_like(out)
    elif half is None:
        out[...] = start[0][...]
    else:
        out[...] = start[0][:, height * half : height * half + height]
    def split_panels(j):
        left = lefts[jobs[j][2]]

        @pl.loop(0, TILES, unroll=4)
        def _(t):
            split_left(left, t)
            if made:
                b3[t] = made[j][t]

        if not made:
            split_right(jobs[j], b3)

    def add_products(s):
        live = counts[s]

        @pl.loop(0, (live + UNROLL - 1) // UNROLL)
        def _(block):
            sums, slots = [], []
            for u in range(UNROLL):
                p = block * UNROLL + u
                c = jnp.dot(a3[pairs[s, 0, p]], b3[pairs[s, 1, p]], preferred_element_type=F32)
                c = c[0 : 2 * height] + c[2 * height : 4 * height]
                sums.append(jnp.where(lane_left, c[0:height], c[height : 2 * height]))
                g = lax.rem(pairs[s, 2, p] + (4 - depth) * 32, SLOTS)
                slots.append(jnp.where(p < live, g, SLOTS))
            for u in range(UNROLL):
                out[slots[u]] += sums[u]

    if len(jobs) == 1:
        split_panels(0)
        add_products(section(jobs[0]))
    else:

        @pl.loop(0, len(jobs))
        def _(now):
            s = jnp.int32(0)
            for j, job in enumerate(jobs):
                s = jnp.where(now == j, section(job), s)
                pl.when(now == j)(functools.partial(split_panels, j))
            add_products(s)

    for job, target in zip(later, splits):
        split_right(job, target)
    for ref, (first, last) in zip(outs, PARTS):
        ref[...] = out[first:last]


def add_sections(jobs, place, pattern, limits, lefts, rights, acc, name, later=[], half=None, made=[]):
    smem = pl.BlockSpec(memory_space=pltpu.SMEM)
    vmem = pl.BlockSpec(memory_space=pltpu.VMEM)
    operands = [*lefts, *rights, *made] + ([] if acc is None else [acc])
    height = 32 if half is None else 16
    sums = (SLOTS + 1, height, 128)
    shapes = [jax.ShapeDtypeStruct(sums, F32)]
    shapes += [jax.ShapeDtypeStruct((TILES, 128, 128), BF16) for _ in later]
    scratch = [pltpu.VMEM((TILES, 4 * height, 128), BF16), pltpu.VMEM((TILES, 128, 128), BF16)]
    if rights:
        scratch.append(pltpu.VMEM((TILES, 64, 128), F32))
    if half is not None:
        shapes = [jax.ShapeDtypeStruct((last - first, height, 128), F32) for first, last in PARTS]
        scratch = [pltpu.VMEM(sums, F32)] + scratch
    out = pl.pallas_call(
        functools.partial(
            section_kernel, jobs, later, len(lefts), len(rights), len(made), acc is not None, half
        ),
        out_shape=shapes,
        in_specs=[smem] * 3 + [vmem] * len(operands),
        out_specs=[vmem] * len(shapes),
        scratch_shapes=scratch,
        compiler_params=pltpu.CompilerParams(vmem_limit_bytes=28 << 20),
        cost_estimate=pl.CostEstimate(flops=0, bytes_accessed=0, transcendentals=0),
        name=name,
    )(place, pattern, limits, *operands)
    return out[0] if len(out) == 1 else out


def reduce_over_depth(parts):
    own, low, up, down, high = parts
    up, down = by_depth(up, 1), by_depth(down, -1)
    up, down = lax.optimization_barrier((up, down))
    up2 = by_depth(low + up[16:32], 1)
    down2 = by_depth(high + down[0:16], -1)
    up2, down2 = lax.optimization_barrier((up2, down2))
    return jnp.concatenate([own[0:16] + down[16:32] + up2, own[16:32] + up[0:16] + down2])


def on_device(left_tiles, right_tiles, square_tiles, pairs, counts):
    row, col = lax.axis_index("row"), lax.axis_index("col")
    core = col % 2
    place = jnp.stack([row % 2 - core, core, lax.axis_index("depth")]).astype(jnp.int32)
    pattern, limits = pairs[0, 0, 0], counts[0, 0, 0]

    right = right_tiles[0, 0, 0, 0].reshape(TILES, 32, 128)
    left = left_tiles[0, 0, 0].reshape(TILES, 32, 128)

    args = (place, pattern, limits)
    choices = [(i, i) for i in range(4)]
    other0 = swap_zh(right)
    same1, same3, same2 = by_y(right, -1), by_y(right, 1), by_y(right, 2)
    twin0 = swap_core(left)
    acc = add_sections([(0, False, 0, [(0, 0)])], *args, [left], [right], None, "sections_a")
    other0, acc, left = lax.optimization_barrier((other0, acc, left))
    halves1 = [by_zl(left[16 * i : 16 * i + 16], -1) for i in range(2)]
    left1 = jnp.concatenate(halves1)
    same1, same3, same2, other0, acc = lax.optimization_barrier((same1, same3, same2, other0, acc))

    other1, other3, other2 = by_y(other0, -1), by_y(other0, 1), by_y(other0, 2)
    halves2 = [by_zl(x, -1) for x in halves1]
    twin1 = swap_core(left1)
    even3, odd3 = (3, False, 0, [(3, 1)]), (3, True, 0, choices)
    acc, made_even = add_sections(
        [(1, False, 0, [(1, 0)])], *args, [left1], [same1, same3], acc, "sections_b", [even3]
    )
    other1, other3, acc, *halves2 = lax.optimization_barrier((other1, other3, acc, *halves2))
    left2 = jnp.concatenate(halves2)

    halves3 = [by_zl(x, -1) for x in halves2]
    jobs = [(2, False, 1, [(2, 3)]), (0, True, 0, [(0, 0), (1, 1), (3, 2)])]
    acc = add_sections(jobs, *args, [twin0, left2], [other0, other1, other3, same2], acc, "sections_c")
    twin2 = swap_core(left2)
    other = [other0, other1, other2, other3]
    jobs = [(k, True, k - 1, choices) for k in (1, 2)]
    acc, made_odd = add_sections(jobs, *args, [twin1, twin2], other, acc, "sections_d", [odd3])

    halves3[0], halves3[1], acc = lax.optimization_barrier((halves3[0], halves3[1], acc))
    left3 = jnp.concatenate(halves3)
    twin3 = swap_core(left3)
    acc = add_sections([even3], *args, [left3], [], acc, "sections_e", made=[made_even])
    share = [
        add_sections([odd3], *args, [twin3], [], acc, f"sections_f{h}", [], h, [made_odd]) for h in range(2)
    ]
    share = [reduce_over_depth(half) for half in share]
    share = jnp.concatenate(share, axis=1)
    purified = 3.0 * square_tiles[0, 0] - 2.0 * share.reshape(TILES, 4096)
    return purified[None, None]


def solution(mesh):
    in_specs = (
        P("row", "col", "depth", None, None),
        P("row", "col", "depth", None, None, None),
        P("row", "col", "depth", None),
        P("row", "col", "depth", None, None, None),
        P("row", "col", "depth", None),
    )
    out_specs = P("row", "col", "depth", None)
    return jax.shard_map(
        on_device, mesh=mesh, in_specs=in_specs, out_specs=out_specs, check_vma=False
    )
```

```python
import functools

import jax
import jax.numpy as jnp
from jax import lax
from jax.experimental import pallas as pl
from jax.experimental.pallas import tpu as pltpu
from jax.sharding import PartitionSpec as P

AXES = ("row", "col", "depth")
F32 = jnp.float32
BF16 = jnp.bfloat16
TILES = 32
SLOTS = 128
UNROLL = 64
PARTS = ((0, 32), (32, 48), (48, 80), (80, 112), (112, 128))


def moved(x, target):
    pairs = []
    for y in range(4):
        for zh in range(2):
            for zl in range(4):
                for c in range(2):
                    for d in range(4):
                        ty, th, tl, tc, td = target(y, zh, zl, c, d)
                        source = ((y * 2 + zh) * 8 + zl * 2 + c) * 4 + d
                        dest = ((ty % 4 * 2 + th % 2) * 8 + tl % 4 * 2 + tc % 2) * 4 + td % 4
                        pairs.append((source, dest))
    return lax.ppermute(x, AXES, pairs)


def by_y(x, k):
    return moved(x, lambda y, zh, zl, c, d: (y + k, zh, zl, c, d))


def by_zl(x, k):
    return moved(x, lambda y, zh, zl, c, d: (y, zh, zl + k, c, d))


def by_depth(x, k):
    return moved(x, lambda y, zh, zl, c, d: (y, zh, zl, c, d + k))


def swap_zh(x):
    return moved(x, lambda y, zh, zl, c, d: (y, zh + 1, zl, c, d))


def swap_core(x):
    return moved(x, lambda y, zh, zl, c, d: (y, zh, zl, c + 1, d))


def split(p):
    high = p.astype(BF16).astype(F32)
    return high, p - high


def section_kernel(jobs, later, n_left, n_right, n_made, has_acc, half, *refs):
    def take(n):
        nonlocal refs
        taken, refs = refs[:n], refs[n:]
        return taken

    place, pairs, counts = take(3)
    lefts, rights, made = take(n_left), take(n_right), take(n_made)
    start = take(1) if has_acc else ()
    outs = take(len(PARTS)) if half is not None else ()
    out = take(1)[0]
    splits = take(len(later))
    a3, b3 = take(2)
    rows = take(1)[0] if rights else None
    shift, core, depth = place[0], place[1], place[2]
    lane = lax.broadcasted_iota(jnp.int32, (32, 128), 1) < 64
    height = out.shape[1]
    lane_left = lane[:height]

    def section(job):
        k, odd = job[0], job[1]
        return lax.rem(2 * k + 9 - 2 * core, 8) if odd else 2 * k

    def split_left(left, t):
        p = left[t] if half is None else left[t, height * half : height * half + height]
        h, low = split(p)
        hr = pltpu.roll(h, 64, 1)
        lr = pltpu.roll(low, 64, 1)
        a3[t, 0:height] = jnp.where(lane_left, h, hr).astype(BF16)
        a3[t, height : 2 * height] = jnp.where(lane_left, hr, h).astype(BF16)
        a3[t, 2 * height : 3 * height] = jnp.where(lane_left, low, lr).astype(BF16)
        a3[t, 3 * height : 4 * height] = jnp.where(lane_left, lr, low).astype(BF16)

    def split_right(job, target):
        k, _, _, choices = job

        def interleave(ref):
            @pl.loop(0, TILES, unroll=4)
            def _(t):
                r = ref[t]
                rr = pltpu.roll(r, 64, 1)
                rows[t, pl.ds(0, 32, stride=2)] = jnp.where(lane, r, rr)
                rows[t, pl.ds(1, 32, stride=2)] = jnp.where(lane, rr, r)

        if len(choices) == 1:
            interleave(rights[choices[0][1]])
        else:
            want = lax.rem(k + shift + 4, 4)
            for offset, index in choices:
                pl.when(want == offset)(functools.partial(interleave, rights[index]))

        @pl.loop(0, TILES, unroll=4)
        def _(t):
            h, low = split(rows[t])
            target[t, 0:64] = h.astype(BF16)
            target[t, 64:128] = low.astype(BF16)

    if not has_acc:
        out[...] = jnp.zeros_like(out)
    elif half is None:
        out[...] = start[0][...]
    else:
        out[...] = start[0][:, height * half : height * half + height]
    def split_panels(j):
        left = lefts[jobs[j][2]]

        @pl.loop(0, TILES, unroll=4)
        def _(t):
            split_left(left, t)
            if made:
                b3[t] = made[j][t]

        if not made:
            split_right(jobs[j], b3)

    def add_products(s):
        live = counts[s]

        @pl.loop(0, (live + UNROLL - 1) // UNROLL)
        def _(block):
            sums, slots = [], []
            for u in range(UNROLL):
                p = block * UNROLL + u
                c = jnp.dot(a3[pairs[s, 0, p]], b3[pairs[s, 1, p]], preferred_element_type=F32)
                c = c[0 : 2 * height] + c[2 * height : 4 * height]
                sums.append(jnp.where(lane_left, c[0:height], c[height : 2 * height]))
                g = lax.rem(pairs[s, 2, p] + (4 - depth) * 32, SLOTS)
                slots.append(jnp.where(p < live, g, SLOTS))
            for u in range(UNROLL):
                out[slots[u]] += sums[u]

    if len(jobs) == 1:
        split_panels(0)
        add_products(section(jobs[0]))
    else:

        @pl.loop(0, len(jobs))
        def _(now):
            s = jnp.int32(0)
            for j, job in enumerate(jobs):
                s = jnp.where(now == j, section(job), s)
                pl.when(now == j)(functools.partial(split_panels, j))
            add_products(s)

    for job, target in zip(later, splits):
        split_right(job, target)
    for ref, (first, last) in zip(outs, PARTS):
        ref[...] = out[first:last]


def add_sections(jobs, place, pattern, limits, lefts, rights, acc, name, later=[], half=None, made=[]):
    smem = pl.BlockSpec(memory_space=pltpu.SMEM)
    vmem = pl.BlockSpec(memory_space=pltpu.VMEM)
    operands = [*lefts, *rights, *made] + ([] if acc is None else [acc])
    height = 32 if half is None else 16
    sums = (SLOTS + 1, height, 128)
    shapes = [jax.ShapeDtypeStruct(sums, F32)]
    shapes += [jax.ShapeDtypeStruct((TILES, 128, 128), BF16) for _ in later]
    scratch = [pltpu.VMEM((TILES, 4 * height, 128), BF16), pltpu.VMEM((TILES, 128, 128), BF16)]
    if rights:
        scratch.append(pltpu.VMEM((TILES, 64, 128), F32))
    if half is not None:
        shapes = [jax.ShapeDtypeStruct((last - first, height, 128), F32) for first, last in PARTS]
        scratch = [pltpu.VMEM(sums, F32)] + scratch
    out = pl.pallas_call(
        functools.partial(
            section_kernel, jobs, later, len(lefts), len(rights), len(made), acc is not None, half
        ),
        out_shape=shapes,
        in_specs=[smem] * 3 + [vmem] * len(operands),
        out_specs=[vmem] * len(shapes),
        scratch_shapes=scratch,
        compiler_params=pltpu.CompilerParams(vmem_limit_bytes=28 << 20),
        cost_estimate=pl.CostEstimate(flops=0, bytes_accessed=0, transcendentals=0),
        name=name,
    )(place, pattern, limits, *operands)
    return out[0] if len(out) == 1 else out


def reduce_over_depth(parts):
    own, low, up, down, high = parts
    up, down = by_depth(up, 1), by_depth(down, -1)
    up, down = lax.optimization_barrier((up, down))
    up2 = by_depth(low + up[16:32], 1)
    down2 = by_depth(high + down[0:16], -1)
    up2, down2 = lax.optimization_barrier((up2, down2))
    return jnp.concatenate([own[0:16] + down[16:32] + up2, own[16:32] + up[0:16] + down2])


def on_device(left_tiles, right_tiles, square_tiles, pairs, counts):
    row, col = lax.axis_index("row"), lax.axis_index("col")
    core = col % 2
    place = jnp.stack([row % 2 - core, core, lax.axis_index("depth")]).astype(jnp.int32)
    pattern, limits = pairs[0, 0, 0], counts[0, 0, 0]

    right = right_tiles[0, 0, 0, 0].reshape(TILES, 32, 128)
    left = left_tiles[0, 0, 0].reshape(TILES, 32, 128)

    args = (place, pattern, limits)
    choices = [(i, i) for i in range(4)]
    other0 = swap_zh(right)
    same1, same3, same2 = by_y(right, -1), by_y(right, 1), by_y(right, 2)
    twin0 = swap_core(left)
    acc = add_sections([(0, False, 0, [(0, 0)])], *args, [left], [right], None, "sections_a")
    other0, acc, left = lax.optimization_barrier((other0, acc, left))
    left1 = by_zl(left, -1)
    same1, same3, same2, other0, acc = lax.optimization_barrier((same1, same3, same2, other0, acc))

    other1, other3, other2 = by_y(other0, -1), by_y(other0, 1), by_y(other0, 2)
    left2 = by_zl(left1, -1)
    twin1 = swap_core(left1)
    even3, odd3 = (3, False, 0, [(3, 1)]), (3, True, 0, choices)
    acc, made_even = add_sections(
        [(1, False, 0, [(1, 0)])], *args, [left1], [same1, same3], acc, "sections_b", [even3]
    )
    other1, other3, left2, acc = lax.optimization_barrier((other1, other3, left2, acc))

    left3 = by_zl(left2, -1)
    jobs = [(2, False, 1, [(2, 3)]), (0, True, 0, [(0, 0), (1, 1), (3, 2)])]
    acc = add_sections(jobs, *args, [twin0, left2], [other0, other1, other3, same2], acc, "sections_c")
    twin2 = swap_core(left2)
    other = [other0, other1, other2, other3]
    jobs = [(k, True, k - 1, choices) for k in (1, 2)]
    acc, made_odd = add_sections(jobs, *args, [twin1, twin2], other, acc, "sections_d", [odd3])

    left3, acc = lax.optimization_barrier((left3, acc))
    twin3 = swap_core(left3)
    acc = add_sections([even3], *args, [left3], [], acc, "sections_e", made=[made_even])
    share = [
        add_sections([odd3], *args, [twin3], [], acc, f"sections_f{h}", [], h, [made_odd]) for h in range(2)
    ]
    share = [reduce_over_depth(half) for half in share]
    share = jnp.concatenate(share, axis=1)
    purified = 3.0 * square_tiles[0, 0] - 2.0 * share.reshape(TILES, 4096)
    return purified[None, None]


def solution(mesh):
    in_specs = (
        P("row", "col", "depth", None, None),
        P("row", "col", "depth", None, None, None),
        P("row", "col", "depth", None),
        P("row", "col", "depth", None, None, None),
        P("row", "col", "depth", None),
    )
    out_specs = P("row", "col", "depth", None)
    return jax.shard_map(
        on_device, mesh=mesh, in_specs=in_specs, out_specs=out_specs, check_vma=False
    )
```

```python
import functools

import jax
import jax.numpy as jnp
from jax import lax
from jax.experimental import pallas as pl
from jax.experimental.pallas import tpu as pltpu
from jax.sharding import PartitionSpec as P

AXES = ("row", "col", "depth")
F32 = jnp.float32
BF16 = jnp.bfloat16
TILES = 32
SLOTS = 128
UNROLL = 64
PARTS = ((0, 32), (32, 48), (48, 80), (80, 112), (112, 128))


def moved(x, target):
    pairs = []
    for y in range(4):
        for zh in range(2):
            for zl in range(4):
                for c in range(2):
                    for d in range(4):
                        ty, th, tl, tc, td = target(y, zh, zl, c, d)
                        source = ((y * 2 + zh) * 8 + zl * 2 + c) * 4 + d
                        dest = ((ty % 4 * 2 + th % 2) * 8 + tl % 4 * 2 + tc % 2) * 4 + td % 4
                        pairs.append((source, dest))
    return lax.ppermute(x, AXES, pairs)


def by_y(x, k):
    return moved(x, lambda y, zh, zl, c, d: (y + k, zh, zl, c, d))


def by_zl(x, k):
    return moved(x, lambda y, zh, zl, c, d: (y, zh, zl + k, c, d))


def by_depth(x, k):
    return moved(x, lambda y, zh, zl, c, d: (y, zh, zl, c, d + k))


def swap_zh(x):
    return moved(x, lambda y, zh, zl, c, d: (y, zh + 1, zl, c, d))


def swap_core(x):
    return moved(x, lambda y, zh, zl, c, d: (y, zh, zl, c + 1, d))


def split(p):
    high = p.astype(BF16).astype(F32)
    return high, p - high


def section_kernel(jobs, later, n_left, n_right, n_made, has_acc, half, *refs):
    def take(n):
        nonlocal refs
        taken, refs = refs[:n], refs[n:]
        return taken

    place, pairs, counts = take(3)
    lefts, rights, made = take(n_left), take(n_right), take(n_made)
    start = take(1) if has_acc else ()
    outs = take(len(PARTS)) if half is not None else ()
    out = take(1)[0]
    splits = take(len(later))
    a3, b3 = take(2)
    rows = take(1)[0] if rights else None
    shift, core, depth = place[0], place[1], place[2]
    lane = lax.broadcasted_iota(jnp.int32, (32, 128), 1) < 64
    height = out.shape[1]
    lane_left = lane[:height]

    def section(job):
        k, odd = job[0], job[1]
        return lax.rem(2 * k + 9 - 2 * core, 8) if odd else 2 * k

    def split_left(left, t):
        p = left[t] if half is None else left[t, height * half : height * half + height]
        h, low = split(p)
        hr = pltpu.roll(h, 64, 1)
        lr = pltpu.roll(low, 64, 1)
        a3[t, 0:height] = jnp.where(lane_left, h, hr).astype(BF16)
        a3[t, height : 2 * height] = jnp.where(lane_left, hr, h).astype(BF16)
        a3[t, 2 * height : 3 * height] = jnp.where(lane_left, low, lr).astype(BF16)
        a3[t, 3 * height : 4 * height] = jnp.where(lane_left, lr, low).astype(BF16)

    def split_right(job, target):
        k, _, _, choices = job

        def interleave(ref):
            @pl.loop(0, TILES, unroll=8)
            def _(t):
                r = ref[t]
                rr = pltpu.roll(r, 64, 1)
                rows[t, pl.ds(0, 32, stride=2)] = jnp.where(lane, r, rr)
                rows[t, pl.ds(1, 32, stride=2)] = jnp.where(lane, rr, r)

        if len(choices) == 1:
            interleave(rights[choices[0][1]])
        else:
            want = lax.rem(k + shift + 4, 4)
            for offset, index in choices:
                pl.when(want == offset)(functools.partial(interleave, rights[index]))

        @pl.loop(0, TILES, unroll=8)
        def _(t):
            h, low = split(rows[t])
            target[t, 0:64] = h.astype(BF16)
            target[t, 64:128] = low.astype(BF16)

    if not has_acc:
        out[...] = jnp.zeros_like(out)
    elif half is None:
        out[...] = start[0][...]
    else:
        out[...] = start[0][:, height * half : height * half + height]
    def split_panels(j):
        left = lefts[jobs[j][2]]

        @pl.loop(0, TILES, unroll=8)
        def _(t):
            split_left(left, t)
            if made:
                b3[t] = made[j][t]

        if not made:
            split_right(jobs[j], b3)

    def add_products(s):
        live = counts[s]

        @pl.loop(0, (live + UNROLL - 1) // UNROLL)
        def _(block):
            sums, slots = [], []
            for u in range(UNROLL):
                p = block * UNROLL + u
                c = jnp.dot(a3[pairs[s, 0, p]], b3[pairs[s, 1, p]], preferred_element_type=F32)
                c = c[0 : 2 * height] + c[2 * height : 4 * height]
                sums.append(jnp.where(lane_left, c[0:height], c[height : 2 * height]))
                g = lax.rem(pairs[s, 2, p] + (4 - depth) * 32, SLOTS)
                slots.append(jnp.where(p < live, g, SLOTS))
            for u in range(UNROLL):
                out[slots[u]] += sums[u]

    if len(jobs) == 1:
        split_panels(0)
        add_products(section(jobs[0]))
    else:

        @pl.loop(0, len(jobs))
        def _(now):
            s = jnp.int32(0)
            for j, job in enumerate(jobs):
                s = jnp.where(now == j, section(job), s)
                pl.when(now == j)(functools.partial(split_panels, j))
            add_products(s)

    for job, target in zip(later, splits):
        split_right(job, target)
    for ref, (first, last) in zip(outs, PARTS):
        ref[...] = out[first:last]


def add_sections(jobs, place, pattern, limits, lefts, rights, acc, name, later=[], half=None, made=[]):
    smem = pl.BlockSpec(memory_space=pltpu.SMEM)
    vmem = pl.BlockSpec(memory_space=pltpu.VMEM)
    operands = [*lefts, *rights, *made] + ([] if acc is None else [acc])
    height = 32 if half is None else 16
    sums = (SLOTS + 1, height, 128)
    shapes = [jax.ShapeDtypeStruct(sums, F32)]
    shapes += [jax.ShapeDtypeStruct((TILES, 128, 128), BF16) for _ in later]
    scratch = [pltpu.VMEM((TILES, 4 * height, 128), BF16), pltpu.VMEM((TILES, 128, 128), BF16)]
    if rights:
        scratch.append(pltpu.VMEM((TILES, 64, 128), F32))
    if half is not None:
        shapes = [jax.ShapeDtypeStruct((last - first, height, 128), F32) for first, last in PARTS]
        scratch = [pltpu.VMEM(sums, F32)] + scratch
    out = pl.pallas_call(
        functools.partial(
            section_kernel, jobs, later, len(lefts), len(rights), len(made), acc is not None, half
        ),
        out_shape=shapes,
        in_specs=[smem] * 3 + [vmem] * len(operands),
        out_specs=[vmem] * len(shapes),
        scratch_shapes=scratch,
        compiler_params=pltpu.CompilerParams(vmem_limit_bytes=28 << 20),
        cost_estimate=pl.CostEstimate(flops=0, bytes_accessed=0, transcendentals=0),
        name=name,
    )(place, pattern, limits, *operands)
    return out[0] if len(out) == 1 else out


def reduce_over_depth(parts):
    own, low, up, down, high = parts
    up, down = by_depth(up, 1), by_depth(down, -1)
    up, down = lax.optimization_barrier((up, down))
    up2 = by_depth(low + up[16:32], 1)
    down2 = by_depth(high + down[0:16], -1)
    up2, down2 = lax.optimization_barrier((up2, down2))
    return jnp.concatenate([own[0:16] + down[16:32] + up2, own[16:32] + up[0:16] + down2])


def on_device(left_tiles, right_tiles, square_tiles, pairs, counts):
    row, col = lax.axis_index("row"), lax.axis_index("col")
    core = col % 2
    place = jnp.stack([row % 2 - core, core, lax.axis_index("depth")]).astype(jnp.int32)
    pattern, limits = pairs[0, 0, 0], counts[0, 0, 0]

    right = right_tiles[0, 0, 0, 0].reshape(TILES, 32, 128)
    left = left_tiles[0, 0, 0].reshape(TILES, 32, 128)

    args = (place, pattern, limits)
    choices = [(i, i) for i in range(4)]
    other0 = swap_zh(right)
    same1, same3, same2 = by_y(right, -1), by_y(right, 1), by_y(right, 2)
    twin0 = swap_core(left)
    acc = add_sections([(0, False, 0, [(0, 0)])], *args, [left], [right], None, "sections_a")
    other0, acc, left = lax.optimization_barrier((other0, acc, left))
    left1 = by_zl(left, -1)
    same1, same3, same2, other0, acc = lax.optimization_barrier((same1, same3, same2, other0, acc))

    other1, other3, other2 = by_y(other0, -1), by_y(other0, 1), by_y(other0, 2)
    left2 = by_zl(left1, -1)
    twin1 = swap_core(left1)
    even3, odd3 = (3, False, 0, [(3, 1)]), (3, True, 0, choices)
    acc, made_even = add_sections(
        [(1, False, 0, [(1, 0)])], *args, [left1], [same1, same3], acc, "sections_b", [even3]
    )
    other1, other3, left2, acc = lax.optimization_barrier((other1, other3, left2, acc))

    left3 = by_zl(left2, -1)
    jobs = [(2, False, 1, [(2, 3)]), (0, True, 0, [(0, 0), (1, 1), (3, 2)])]
    acc = add_sections(jobs, *args, [twin0, left2], [other0, other1, other3, same2], acc, "sections_c")
    twin2 = swap_core(left2)
    other = [other0, other1, other2, other3]
    jobs = [(k, True, k - 1, choices) for k in (1, 2)]
    acc, made_odd = add_sections(jobs, *args, [twin1, twin2], other, acc, "sections_d", [odd3])

    left3, acc = lax.optimization_barrier((left3, acc))
    twin3 = swap_core(left3)
    acc = add_sections([even3], *args, [left3], [], acc, "sections_e", made=[made_even])
    share = [
        add_sections([odd3], *args, [twin3], [], acc, f"sections_f{h}", [], h, [made_odd]) for h in range(2)
    ]
    share = [reduce_over_depth(half) for half in share]
    share = jnp.concatenate(share, axis=1)
    purified = 3.0 * square_tiles[0, 0] - 2.0 * share.reshape(TILES, 4096)
    return purified[None, None]


def solution(mesh):
    in_specs = (
        P("row", "col", "depth", None, None),
        P("row", "col", "depth", None, None, None),
        P("row", "col", "depth", None),
        P("row", "col", "depth", None, None, None),
        P("row", "col", "depth", None),
    )
    out_specs = P("row", "col", "depth", None)
    return jax.shard_map(
        on_device, mesh=mesh, in_specs=in_specs, out_specs=out_specs, check_vma=False
    )
```
